256 devices in a mesh: section: 2 (over x_hi), expert: 128 (over z, y, x_lo, core).
Axes of the slice: x: 4 (x_hi: 2, x_lo: 2; x = x_hi * 2 + x_lo), y: 4, z: 8, core: 2. Of those that a mesh axis runs over, the one named last changes fastest.
Arguments:
- tokens: bfloat16 [16384, 2048], P('expert'), may hold values from -6 to 6
- memory: bfloat16 [256, 32, 2, 2048], P('expert', 'section'), may hold values from -51 to 51
- target_len: int32 [256], P('expert'), may hold values from 32 to 64
- source_len: int32 [256], P('expert'), may hold values from 8 to 32
- attn_gain: float32 [2048], replicated, may hold values from 0.5 to 1.5
- w_query: bfloat16 [2048, 2048], P('expert', 'section'), may hold values from -0.125 to 0.125
- w_out: bfloat16 [2048, 2048], P('section', 'expert'), may hold values from -0.125 to 0.125
- moe_gain: float32 [2048], replicated, may hold values from 0.5 to 1.5
- w_router: bfloat16 [2048, 64], replicated, may hold values from -0.125 to 0.125
- expert_ids: int32 [16384, 2], P('expert'), may hold values from 0 to 63, all different within a row; in each aligned block of 128 rows (0 to 127, 128 to 255, ...) at most 6 rows name the same one
- w_up: bfloat16 [128, 2048, 2048], P('expert', None, 'section'), may hold values from -0.125 to 0.125
- w_down: bfloat16 [128, 2048, 2048], P('expert', 'section'), may hold values from -0.09375 to 0.09375
Outputs:
- layer_out: bfloat16 [16384, 2048], P('expert')
The draws below stay inside these ranges and needn't reach their ends.
Inputs may be any that keep to these rules, and one draw needn't show every extreme that they name: `expert_ids`: within the 128 tokens of one index of the expert axis, no expert is named by more than 6 tokens, a bound that some block reaches; the two experts of a token differ.
All inputs are finite; a program needn't handle non-finite values.
Results may differ from the reference program's by a relative error of at most 0.015.
Values may be sent and summed in bfloat16 or wider, within the bound.
A program may use at most 64 MiB of HBM per device.

```python
import math
import jax
import jax.numpy as jnp
import numpy as np
from jax import lax

D = 2048
HEADS = 16
HD = 128
FF = 4096
TGT_LEN = 64
SRC_LEN = 32
TOK_DEV = 128
SEQS = 256
TOKENS = 16384
EXPERTS = 64
CAP = 6
N_EXPERT = 128


def draw_memory(key, part):
    key = jax.random.fold_in(key, 5)
    first_key = jax.random.fold_in(key, 0)
    shape = (SEQS, SRC_LEN, 2, HEADS * HD)
    base = jnp.clip(jax.random.normal(first_key, shape, jnp.float32), -6.0, 6.0)
    return base.astype(jnp.bfloat16)


def place_ends(entries, stream_key, smallest, high):
    spot = [jax.random.randint(jax.random.fold_in(stream_key, axis), (), 0, length) for axis, length in enumerate(entries.shape)]
    longest = entries.shape.index(max(entries.shape))
    neighbour = spot[:longest] + [(spot[longest] + 1) % entries.shape[longest]] + spot[longest + 1:]
    return entries.at[tuple(spot)].set(smallest).at[tuple(neighbour)].set(high)


def block_scale(own_key, extent, pieces, low, top_value):
    factor_of, own = 1.0, jax.random.fold_in(own_key, 6)
    for position, shards_of in pieces:
        steps = jnp.exp(jax.random.uniform(jax.random.fold_in(own, position), (shards_of,), jnp.float32, low / len(pieces), top_value / len(pieces)))
        factor_of = factor_of * jnp.repeat(steps, extent[position] // shards_of).reshape([-1 if axis == position else 1 for axis in range(len(extent))])
    return factor_of


def shared_out(key, own, number, rows, count, top, limit, skew):
    order = jax.random.permutation(key, count)
    crowded, common = shares(count, rows * top, limit, skew, True), shares(count, rows * top, limit, skew, False)
    places = jnp.arange(count)

    def named(tallies, offset_by):
        used = int((tallies > 0).sum())
        fixed = max(1, used // 4)
        shifted = fixed + (places - fixed + offset_by * (used - fixed)) % max(1, count - fixed)
        return jnp.zeros((count,), jnp.int32).at[order[jnp.where(places < fixed, places, shifted)]].set(jnp.asarray(tallies, jnp.int32))

    tallies = jnp.where(number % 4 == 0, named(crowded, number // 4), named(common, number - number // 4 - 1))
    mixed = jax.random.permutation(jax.random.fold_in(own, 3), count)
    giver, taker = mixed[0:count // 2 * 2:2], mixed[1:count // 2 * 2:2]
    slack = jnp.minimum(tallies[giver] - 1, limit - tallies[taker]) // 2
    slack = jnp.where((giver == order[0]) | (taker == order[0]) | (tallies[taker] == 0), 0, jnp.maximum(slack, 0))
    shifted = jax.random.randint(jax.random.fold_in(own, 4), (count // 2,), 0, 1 << 20) % (slack + 1)
    tallies = tallies.at[giver].add(-shifted).at[taker].add(shifted)
    members = jnp.searchsorted(jnp.cumsum(tallies), jnp.arange(rows * top), side="right").astype(jnp.int32)
    grid = members.reshape(top, rows).T
    grid = grid[jax.random.permutation(jax.random.fold_in(own, 1), rows)]
    offset_by = jax.random.randint(jax.random.fold_in(own, 2), (rows, 1), 0, top)
    return jnp.take_along_axis(grid, (jnp.arange(top)[None, :] + offset_by) % top, axis=1)


def shares(count, total, limit, slope, full):
    weights = [(1 << 20) // math.isqrt(grade ** slope) + 1 for grade in range(1, count + 1)]
    largest = limit if full else min(limit, max(-(-total // count), total * weights[0] // sum(weights)))
    least = 1 if total - largest >= count - 1 else 0
    given, rest = [largest] + [least] * (count - 1), total - largest - least * (count - 1)
    while rest > 0:
        candidates = [i for i in range(1, count) if given[i] < largest] or [i for i in range(1, count) if given[i] < limit]
        mass, budget = sum([weights[i] for i in candidates]), rest
        for i in candidates:
            extra = min(limit - given[i], max(1, budget * weights[i] // mass), rest)
            given[i] = given[i] + extra
            rest = rest - extra
    return np.array(given)


def scatter_about(rng, dims, scale, most, pieces=(), held_as=jnp.bfloat16):
    result = jax.random.normal(rng, dims, jnp.float32) * scale
    if len(pieces) > 0:
        result = block_scale(rng, dims, pieces, -0.22, 0.18) * result
    return jnp.clip(result, min=-most, max=most).astype(held_as)


def setup_inputs(seed: int = 0) -> dict:
    key_list = jax.random.split(jax.random.key(seed), 13)
    tokens = scatter_about(key_list[0], (TOKENS, D), 1.0, 6.0, ((0, 128),))
    memory = draw_memory(jax.random.fold_in(key_list[12], 71), 0)
    target_len = place_ends(jax.random.randint(key_list[2], (SEQS,), TGT_LEN // 2, TGT_LEN + 1), jax.random.fold_in(key_list[2], 1), TGT_LEN // 2, TGT_LEN).astype(jnp.int32)
    source_len = place_ends(jax.random.randint(key_list[3], (SEQS,), SRC_LEN // 4, SRC_LEN + 1), jax.random.fold_in(key_list[3], 1), SRC_LEN // 4, SRC_LEN).astype(jnp.int32)
    attn_gain = jnp.clip(1.0 + 0.1 * jax.random.normal(key_list[4], (D,), jnp.float32), 0.5, 1.5)
    w_query = scatter_about(key_list[5], (D, HEADS * HD), D ** -0.5, 0.125, ((0, 128), (1, 2)))
    w_out = scatter_about(key_list[6], (HEADS * HD, D), (HEADS * HD) ** -0.5, 0.125, ((0, 2), (1, 128)))
    moe_gain = jnp.clip(1.0 + 0.1 * jax.random.normal(key_list[7], (D,), jnp.float32), 0.5, 1.5)
    w_router = scatter_about(key_list[8], (D, EXPERTS), D ** -0.5, 0.125)
    expert_ids_keys = jax.random.split(jax.random.fold_in(key_list[9], 1), TOKENS // TOK_DEV)
    expert_ids_turns = jax.random.permutation(jax.random.fold_in(key_list[9], 3), TOKENS // TOK_DEV)
    expert_ids = jax.vmap(lambda own, number: shared_out(jax.random.fold_in(key_list[9], 2), own, number, TOK_DEV, EXPERTS, 2, CAP, 2))(expert_ids_keys, expert_ids_turns).reshape((TOKENS, 2))
    w_up = scatter_about(key_list[10], (N_EXPERT, D, FF // 2), D ** -0.5, 0.125, ((0, 128), (2, 2)))
    w_down = scatter_about(key_list[11], (N_EXPERT, FF // 2, D), FF ** -0.5, 0.09375, ((0, 128), (1, 2)))
    return dict(tokens=tokens, memory=memory, target_len=target_len, source_len=source_len, attn_gain=attn_gain, w_query=w_query, w_out=w_out, moe_gain=moe_gain, w_router=w_router, expert_ids=expert_ids, w_up=w_up, w_down=w_down)


def layer_norm(values, gain):
    center = values - lax.optimization_barrier(jnp.mean(values, axis=-1, keepdims=True))
    spread = lax.optimization_barrier(jnp.mean(center * center, axis=-1, keepdims=True))
    return center * lax.rsqrt(spread + 1e-05) * gain

def assign_slots(expert_ids, live_rows, experts, capacity):
    flat_ids = expert_ids.reshape(-1)
    alive_rows = jnp.repeat(live_rows, 2)
    onehot = ((flat_ids[:, None] == jnp.arange(experts, dtype=jnp.int32)[None, :]) & alive_rows[:, None]).astype(jnp.int32)
    before = jnp.cumsum(onehot, axis=0) - onehot
    slot_index = lax.optimization_barrier(jnp.sum(before * onehot, axis=1)).astype(jnp.int32)
    target = jnp.where(alive_rows, flat_ids * capacity + slot_index, -1).astype(jnp.int32)
    return target.reshape(expert_ids.shape)

def reference(tokens, memory, target_len, source_len, attn_gain, w_query, w_out, moe_gain, w_router, expert_ids, w_up, w_down):
    residual_in = tokens.astype(jnp.float32)
    normed = layer_norm(residual_in, attn_gain).astype(jnp.bfloat16)
    query = jnp.dot(normed, w_query, preferred_element_type=jnp.float32).astype(jnp.bfloat16)
    query_heads = query.reshape(SEQS, TGT_LEN, HEADS, HD).astype(jnp.float32)
    key_heads = memory[:, :, 0].reshape(SEQS, SRC_LEN, HEADS, HD).astype(jnp.float32)
    value_heads = memory[:, :, 1].reshape(SEQS, SRC_LEN, HEADS, HD).astype(jnp.float32)
    scores = jnp.einsum('sqhd,skhd->shqk', query_heads, key_heads) * HD ** (-0.5)
    visible = jnp.arange(SRC_LEN, dtype=jnp.int32)[None, :] < source_len[:, None]
    scores = jnp.where(visible[:, None, None, :], scores, -1e+30)
    weights = jax.nn.softmax(scores, axis=-1).astype(jnp.bfloat16)
    context = jnp.einsum('shqk,skhd->sqhd', weights.astype(jnp.float32), value_heads).astype(jnp.bfloat16)
    context = context.reshape(TOKENS, HEADS * HD)
    after_attn = residual_in + jnp.dot(context, w_out, preferred_element_type=jnp.float32)
    moe_in = layer_norm(after_attn, moe_gain).astype(jnp.bfloat16)
    logits = jnp.dot(moe_in, w_router, preferred_element_type=jnp.float32)
    picked = jnp.take_along_axis(logits, expert_ids, axis=1)
    gates = jax.nn.sigmoid(picked - picked[:, ::-1])
    live_rows = (jnp.arange(TGT_LEN, dtype=jnp.int32)[None, :] < target_len[:, None]).reshape(-1)
    targets = jax.vmap(lambda ids_dev, live_dev: assign_slots(ids_dev, live_dev, EXPERTS, CAP))(expert_ids.reshape(N_EXPERT, TOK_DEV, 2), live_rows.reshape(N_EXPERT, TOK_DEV))
    row_numbers = jnp.repeat(jnp.arange(TOK_DEV, dtype=jnp.int32), 2)

    def device_table(target_dev):
        where_to = jnp.where(target_dev.reshape(-1) < 0, EXPERTS * CAP, target_dev.reshape(-1))
        empty = jnp.full((EXPERTS * CAP,), TOK_DEV, jnp.int32)
        return empty.at[where_to].set(row_numbers, mode='drop')
    table = jax.vmap(device_table)(targets)
    padded_rows = jnp.concatenate([moe_in.reshape(N_EXPERT, TOK_DEV, D), jnp.zeros((N_EXPERT, 1, D), jnp.bfloat16)], axis=1)
    quarter = FF // 4

    def run_expert(expert_index):
        slot_rows = lax.dynamic_slice_in_dim(table, expert_index * CAP, CAP, 1)
        rows = jnp.take_along_axis(padded_rows, slot_rows[:, :, None], axis=1).reshape(N_EXPERT * CAP, D)
        up_pair = lax.dynamic_slice_in_dim(w_up, expert_index * 2, 2, 0)
        down_pair = lax.dynamic_slice_in_dim(w_down, expert_index * 2, 2, 0)
        total = jnp.zeros((N_EXPERT * CAP, D), jnp.float32)
        for part_index in range(2):
            pair_total = jnp.zeros((N_EXPERT * CAP, D), jnp.float32)
            for half_index in range(2):
                up_block = up_pair[half_index][:, part_index * quarter:(part_index + 1) * quarter]
                down_block = down_pair[half_index][part_index * quarter:(part_index + 1) * quarter]
                hidden = jnp.maximum(jnp.dot(rows, up_block, preferred_element_type=jnp.float32), 0.0).astype(jnp.bfloat16)
                part_out = jnp.dot(hidden, down_block, preferred_element_type=jnp.float32).astype(jnp.bfloat16)
                part_out = lax.optimization_barrier(part_out)
                pair_total = pair_total + part_out.astype(jnp.float32)
            half_out = lax.optimization_barrier(pair_total.astype(jnp.bfloat16))
            total = total + half_out.astype(jnp.float32)
        return total.reshape(N_EXPERT, CAP, D)
    results = lax.map(run_expert, jnp.arange(EXPERTS, dtype=jnp.int32))
    safe_targets = jnp.where(targets < 0, 0, targets).astype(jnp.int32)
    expert_index = safe_targets // CAP
    slot_index = safe_targets % CAP
    device_index = jnp.arange(N_EXPERT, dtype=jnp.int32)[:, None, None]
    picks = results[expert_index, device_index, slot_index]
    gate_weight = jnp.where(targets < 0, 0.0, gates.reshape(N_EXPERT, TOK_DEV, 2)).astype(jnp.float32)
    moe_out = lax.optimization_barrier(jnp.sum(picks * gate_weight[..., None], axis=2)).reshape(TOKENS, D)
    return (after_attn + moe_out).astype(jnp.bfloat16)
```

```python
import functools

import jax
import jax.numpy as jnp
import numpy as np
from jax import lax
from jax.experimental import pallas as pl
from jax.experimental.pallas import tpu as pltpu
from jax.sharding import PartitionSpec as P

MESH = pl.DeviceIdType.MESH
F32 = jnp.float32
BF16 = jnp.bfloat16

HD = 128
D = 2048
HALF = 1024
TOK = 128
CAP = 6
EXPERTS = 64
SLOTS = EXPERTS * CAP
BLOCK = 8 * CAP
CHUNKS = 2
CW = HALF // CHUNKS
NZ, NY, NX = 8, 4, 2


def coords():
    s = lax.axis_index("section")
    e = lax.axis_index("expert")
    return s, e // 16, (e // 4) % 4, (e // 2) % 2, e % 2


def device(s, z, y, x, c):
    return (s, ((z * NY + y) * NX + x) * 2 + c)


class Net:
    def __init__(self, send_sem, recv_sem):
        self.send_sem, self.recv_sem = send_sem, recv_sem
        self.copies = []

    def send(self, src, dst, target):
        k = len(self.copies)
        copy = pltpu.make_async_remote_copy(
            src_ref=src,
            dst_ref=dst,
            send_sem=self.send_sem.at[k],
            recv_sem=self.recv_sem.at[k],
            device_id=target,
            device_id_type=MESH,
        )
        copy.start()
        self.copies.append(copy)
        return copy

    def finish(self):
        for copy in self.copies:
            copy.wait_send()


def recv(copies):
    for copy in copies:
        copy.wait_recv()


def gather_z_last(net, buf, cols, forwards):
    s, z, y, x, c = coords()
    view = lambda *idx: buf.at[(*idx, slice(None), cols)]
    sibling = device(s, z, y, x, 1 - c)
    mine = view(z, y * 2 + x, c)
    a = net.send(mine, mine, device(s, z, y, 1 - x, c))
    yield
    recv([a])
    pair = view(z, pl.ds(y * 2, 2), c)
    b = [net.send(pair, pair, device(s, z, (y + d) % NY, x, c)) for d in (1, 3, 2)]
    yield
    recv(b)
    slab = view(z, slice(None), c)
    up, down = device(s, (z + 1) % NZ, y, x, c), device(s, (z + 7) % NZ, y, x, c)
    u, d = net.send(slab, slab, up), net.send(slab, slab, down)
    forwards.append(net.send(slab, slab, sibling))
    for step in range(1, 4):
        yield
        recv([u])
        block = view((z + 8 - step) % NZ, slice(None), c)
        part = block if step < 3 else view((z + 8 - step) % NZ, pl.ds(0, 4), c)
        u = net.send(part, part, up)
        forwards.append(net.send(block, block, sibling))
        recv([d])
        block = view((z + step) % NZ, slice(None), c)
        part = block if step < 3 else view((z + step) % NZ, pl.ds(4, 4), c)
        d = net.send(part, part, down)
        forwards.append(net.send(block, block, sibling))
    yield
    recv([u, d])
    block = view((z + 4) % NZ, slice(None), c)
    forwards.append(net.send(block, block, sibling))


def gather_y_last(net, buf, cols, forwards):
    s, z, y, x, c = coords()
    view = lambda *idx: buf.at[(*idx, slice(None), cols)]
    sibling = device(s, z, y, x, 1 - c)
    mine = view(z, y * 2 + x, c)
    a = [net.send(mine, mine, device(s, (z + d) % NZ, y, x, c)) for d in (1, 7, 2, 6, 3, 5, 4)]
    yield
    recv(a)
    line = view(slice(None), y * 2 + x, c)
    b = net.send(line, line, device(s, z, y, 1 - x, c))
    yield
    recv([b])
    up, down = device(s, z, (y + 1) % NY, x, c), device(s, z, (y + 3) % NY, x, c)
    slab = view(slice(None), pl.ds(y * 2, 2), c)
    u, d = net.send(slab, slab, up), net.send(slab, slab, down)
    forwards.append(net.send(slab, slab, sibling))
    yield
    recv([u])
    below = ((y + 3) % NY) * 2
    part = view(pl.ds(0, 4), pl.ds(below, 2), c)
    u = net.send(part, part, up)
    block = view(slice(None), pl.ds(below, 2), c)
    forwards.append(net.send(block, block, sibling))
    recv([d])
    above = ((y + 1) % NY) * 2
    part = view(pl.ds(4, 4), pl.ds(above, 2), c)
    d = net.send(part, part, down)
    block = view(slice(None), pl.ds(above, 2), c)
    forwards.append(net.send(block, block, sibling))
    yield
    recv([u, d])
    block = view(slice(None), pl.ds(((y + 2) % NY) * 2, 2), c)
    forwards.append(net.send(block, block, sibling))


def iota(shape, dim):
    return lax.broadcasted_iota(jnp.int32, shape, dim)


def nt_dot(a, b):
    return lax.dot_general(a, b, (((1,), (1,)), ((), ())), preferred_element_type=F32)


def dot(a, b):
    return jnp.dot(a, b, preferred_element_type=F32)


def kernel(
    tokens_ref,
    memory_ref,
    target_len_ref,
    source_len_ref,
    attn_gain_ref,
    w_query_ref,
    w_out_ref,
    moe_gain_ref,
    w_router_ref,
    ids_ref,
    ids_t_ref,
    perm_ref,
    perm_kv_ref,
    w_up_hbm,
    w_down_hbm,
    out_ref,
    wq,
    wo,
    w_up,
    w_down,
    mem,
    kv,
    normed,
    query_acc,
    context,
    head_send,
    head_recv,
    after,
    stat_send,
    stat_recv,
    logit_send,
    logit_recv,
    table,
    z_send,
    z_recv,
    p_send,
    rows,
    acc,
    hidden,
    part_send,
    part_recv,
    part_own,
    sec_send,
    sec_recv,
    rp_send,
    rp_recv,
    rz_send,
    rz_recv,
    out_send,
    out_recv,
    send_sem,
    recv_sem,
    load_sem,
):
    s, z, y, x, c = coords()
    chip = y * 2 + x
    sibling, partner = device(s, z, y, x, 1 - c), device(1 - s, z, y, x, c)
    z_peers = [device(s, (z + d) % NZ, y, x, c) for d in (4, 3, 5, 2, 6, 1, 7)]
    plane = [(1, 1), (3, 1), (2, 1), (2, 0), (0, 1), (1, 0), (3, 0)]
    p_peers = [device(s, z, (y + dy) % NY, (x + dx) % NX, c) for dy, dx in plane]
    p_chips = [((y + dy) % NY) * 2 + (x + dx) % NX for dy, dx in plane]

    load_up = pltpu.make_async_copy(w_up_hbm, w_up, load_sem.at[0])
    load_down = pltpu.make_async_copy(w_down_hbm, w_down, load_sem.at[1])
    load_up.start()
    load_down.start()

    barrier = pltpu.get_barrier_semaphore()
    peers = [sibling, partner, *z_peers, *p_peers]
    for peer in peers:
        pl.semaphore_signal(barrier, inc=1, device_id=peer, device_id_type=MESH)
    wq[z, chip, c] = w_query_ref[...]
    wo[z, chip, c] = w_out_ref[...]
    pl.semaphore_wait(barrier, len(peers))

    net = Net(send_sem, recv_sem)
    col0 = pl.multiple_of(s * HALF, HALF)
    col1 = pl.multiple_of((1 - s) * HALF, HALF)
    full = pl.ds(0, HALF)
    q_forwards, o_forwards = [], []
    gather_q = gather_z_last(net, wq, full, q_forwards)
    gather_o = gather_y_last(net, wo, full, o_forwards)
    next(gather_q)
    next(gather_o)
    mem_copy = net.send(memory_ref.at[:, pl.ds(col1, HALF)], mem.at[s], partner)
    mem[s] = memory_ref[:, pl.ds(col0, HALF)]

    next(gather_q)

    values = tokens_ref[...].astype(F32)
    center = values - jnp.mean(values, axis=-1, keepdims=True)
    spread = jnp.mean(center * center, axis=-1, keepdims=True)
    normed[...] = (center * lax.rsqrt(spread + 1e-05) * attn_gain_ref[...]).astype(BF16)

    next(gather_o)
    next(gather_q)

    tl0, tl1 = target_len_ref[0], target_len_ref[1]
    t = iota((1, TOK), 1)
    live = t < jnp.where(t < 64, tl0, tl1 + 64)
    i0, i1 = ids_t_ref[0:1, :], ids_t_ref[1:2, :]
    experts = iota((EXPERTS, TOK), 0)
    hit0, hit1 = (experts == i0) & live, (experts == i1) & live
    earlier = (iota((TOK, TOK), 0) < iota((TOK, TOK), 1)).astype(F32).astype(BF16)
    before = dot((hit0.astype(F32) + hit1.astype(F32)).astype(BF16), earlier)
    slot0 = jnp.sum(jnp.where(hit0, before, 0.0), axis=0, keepdims=True)
    slot1 = jnp.sum(jnp.where(hit1, before, 0.0), axis=0, keepdims=True)
    to0 = jnp.where(live, i0.astype(F32) * CAP + slot0, -1.0)
    to1 = jnp.where(live, i1.astype(F32) * CAP + slot1, -1.0)
    places = iota((SLOTS, TOK), 0).astype(F32)
    table[...] = ((places == to0) | (places == to1)).astype(F32).astype(BF16)

    t = iota((TOK, 1), 0)
    live = t < jnp.where(t < 64, tl0, tl1 + 64)
    i0, i1 = ids_ref[:, 0:1], ids_ref[:, 1:2]
    experts = iota((TOK, EXPERTS), 1)
    pick0, pick1 = experts == i0, experts == i1
    hit0, hit1 = pick0 & live, pick1 & live
    earlier = (iota((TOK, TOK), 1) < iota((TOK, TOK), 0)).astype(F32).astype(BF16)
    before = dot(earlier, (hit0.astype(F32) + hit1.astype(F32)).astype(BF16))
    slot0 = jnp.sum(jnp.where(hit0, before, 0.0), axis=1, keepdims=True)
    slot1 = jnp.sum(jnp.where(hit1, before, 0.0), axis=1, keepdims=True)
    from0 = jnp.where(live, i0.astype(F32) * CAP + slot0, -1.0)
    from1 = jnp.where(live, i1.astype(F32) * CAP + slot1, -1.0)

    next(gather_o)
    next(gather_q)
    recv([mem_copy])
    kv[...] = dot(perm_kv_ref[...], mem[...].reshape(TOK, HALF)).astype(BF16)
    next(gather_q)
    next(gather_o)
    next(gather_q)
    for _ in gather_o:
        pass
    for _ in gather_q:
        pass
    recv(q_forwards)

    query_acc[...] = jnp.zeros_like(query_acc)

    @pl.loop(0, NZ)
    def _(k):
        columns = pl.ds(pl.multiple_of(k * 256, 256), 256)
        query_acc[...] += dot(normed[:, columns], wq[k].reshape(256, HALF))

    sl0, sl1 = source_len_ref[0], source_len_ref[1]
    q_row, k_col = iota((TOK, 64), 0), iota((TOK, 64), 1)
    visible = (k_col >= jnp.where(q_row < 64, 0, 32)) & (
        k_col < jnp.where(q_row < 64, sl0, sl1 + 32)
    )
    for h in range(HALF // HD):
        head = slice(h * HD, (h + 1) * HD)
        query = query_acc[:, head].astype(BF16)
        scores = nt_dot(query, kv[0:64, head]) * HD ** (-0.5)
        scores = jnp.where(visible, scores, -1e30)
        scores = jnp.exp(scores - jnp.max(scores, axis=-1, keepdims=True))
        weights = (scores / jnp.sum(scores, axis=-1, keepdims=True)).astype(BF16)
        context[:, head] = dot(weights, kv[64:128, head]).astype(BF16)

    recv(o_forwards)
    for ch in range(CHUNKS):
        other = wo[pl.ds((1 - s) * 4 + 2 * ch, 2)].reshape(CW, HALF)
        head_send[ch] = nt_dot(context[...], other).astype(BF16)
        copy = net.send(head_send.at[ch], head_recv.at[ch], partner)
        head_copies = [copy] if ch == 0 else head_copies + [copy]
    for ch in range(CHUNKS):
        own = wo[pl.ds(s * 4 + 2 * ch, 2)].reshape(CW, HALF)
        columns = pl.ds(pl.multiple_of(s * HALF + ch * CW, CW), CW)
        after[:, ch * CW : (ch + 1) * CW] = tokens_ref[:, columns].astype(F32) + nt_dot(context[...], own)
    for ch in range(CHUNKS):
        recv([head_copies[ch]])
        after[:, ch * CW : (ch + 1) * CW] += head_recv[ch].astype(F32)

    values = after[...]
    mean = jnp.mean(values, axis=-1, keepdims=True)
    center = values - mean
    square = jnp.sum(center * center, axis=-1, keepdims=True)
    stat_send[...] = jnp.where(iota((TOK, 128), 1) < 64, mean, square)
    stat_copy = net.send(stat_send, stat_recv, partner)
    recv([stat_copy])
    mean_other, square_other = stat_recv[:, 0:1], stat_recv[:, 64:65]
    gap = mean - mean_other
    spread = (square + square_other + gap * gap * (HALF / 2)) * (1.0 / D)
    mean = (mean + mean_other) * 0.5
    moe_in = (
        (values - mean) * lax.rsqrt(spread + 1e-05) * moe_gain_ref[:, pl.ds(col0, HALF)]
    ).astype(BF16)

    own_z = pl.ds(pl.multiple_of(z * BLOCK, 16), BLOCK)
    z_copies = []
    for ch in range(CHUNKS):
        z_send[ch] = dot(table[...], moe_in[:, ch * CW : (ch + 1) * CW]).astype(BF16)
        copies = []
        for k, d in enumerate((4, 3, 5, 2, 6, 1, 7)):
            there = pl.ds(pl.multiple_of((z + d) % NZ * BLOCK, 16), BLOCK)
            copies.append(net.send(z_send.at[ch, there], z_recv.at[ch, own_z], z_peers[k]))
        z_recv[ch, own_z] = z_send[ch, own_z]
        z_copies.append(copies)

    logit_send[...] = jnp.zeros_like(logit_send)
    logit_send[:, 0:EXPERTS] = dot(moe_in, w_router_ref[pl.ds(col0, HALF), :])
    logit_copy = net.send(logit_send, logit_recv, partner)

    own_chip = pl.ds(pl.multiple_of(chip * BLOCK, 16), BLOCK)
    p_copies = []
    for ch in range(CHUNKS):
        recv(z_copies[ch])
        p_send[ch] = dot(perm_ref[...], z_recv[ch]).astype(BF16)
        copies = []
        for k, there in enumerate(p_chips):
            block = pl.ds(pl.multiple_of(there * BLOCK, 16), BLOCK)
            copies.append(
                net.send(p_send.at[ch, block], rows.at[c, s, ch, own_chip], p_peers[k])
            )
        rows[c, s, ch, own_chip] = p_send[ch, own_chip]
        p_copies.append(copies)

    load_up.wait()

    def add_up(cc, ss, ch, first):
        depth = pl.ds(pl.multiple_of(ss * HALF + ch * CW, CW), CW)

        @pl.loop(0, HALF // 256)
        def _(n):
            tile = pl.ds(pl.multiple_of(n * 256, 256), 256)
            product = dot(rows[cc, ss, ch], w_up[depth, tile])
            if first:
                acc[cc, :, tile] = product
            else:
                acc[cc, :, tile] += product

    s_copies, own_forwards, other_forwards = [], [], []
    for ch in range(CHUNKS):
        recv(p_copies[ch])
        mine = rows.at[c, s, ch]
        s_copies.append(net.send(mine, mine, partner))
        own_forwards.append(net.send(mine, mine, sibling))
        add_up(c, s, ch, ch == 0)
    for ch in range(CHUNKS):
        recv([own_forwards[ch]])
        add_up(1 - c, s, ch, ch == 0)
    for ch in range(CHUNKS):
        recv([s_copies[ch]])
        theirs = rows.at[c, 1 - s, ch]
        other_forwards.append(net.send(theirs, theirs, sibling))
        add_up(c, 1 - s, ch, False)
    hidden[c] = jnp.maximum(acc[c], 0.0).astype(BF16)
    for ch in range(CHUNKS):
        recv([other_forwards[ch]])
        add_up(1 - c, 1 - s, ch, False)
    hidden[1 - c] = jnp.maximum(acc[1 - c], 0.0).astype(BF16)

    load_down.wait()

    def down(cc, q, into):
        half = 1 - s if q < CHUNKS else s
        start = half * HALF + (q % CHUNKS) * CW
        for n in range(CW // 256):
            tile = pl.ds(pl.multiple_of(start + n * 256, 256), 256)
            into[q, :, n * 256 : (n + 1) * 256] = dot(hidden[cc], w_down[:, tile]).astype(BF16)

    part_copies = []
    for q in range(2 * CHUNKS):
        down(1 - c, q, part_send)
        part_copies.append(net.send(part_send.at[q], part_recv.at[q], sibling))
        down(c, q, part_own)
    sec_copies = []
    for q in range(CHUNKS):
        recv([part_copies[q]])
        sec_send[q] = (part_own[q].astype(F32) + part_recv[q].astype(F32)).astype(BF16)
        sec_copies.append(net.send(sec_send.at[q], sec_recv.at[q], partner))

    rp_copies = []
    for ch in range(CHUNKS):
        q = CHUNKS + ch
        recv([part_copies[q]])
        half_out = (part_own[q].astype(F32) + part_recv[q].astype(F32)).astype(BF16)
        recv([sec_copies[ch]])
        rp_send[ch] = (half_out.astype(F32) + sec_recv[ch].astype(F32)).astype(BF16)
        copies = []
        for k, there in enumerate(p_chips):
            block = pl.ds(pl.multiple_of(there * BLOCK, 16), BLOCK)
            copies.append(net.send(rp_send.at[ch, block], rp_recv.at[ch, own_chip], p_peers[k]))
        rp_recv[ch, own_chip] = rp_send[ch, own_chip]
        rp_copies.append(copies)

    rz_copies = []
    for ch in range(CHUNKS):
        recv(rp_copies[ch])
        rz_send[ch] = dot(perm_ref[...], rp_recv[ch]).astype(BF16)
        copies = []
        for k, d in enumerate((4, 3, 5, 2, 6, 1, 7)):
            there = pl.ds(pl.multiple_of((z + d) % NZ * BLOCK, 16), BLOCK)
            copies.append(net.send(rz_send.at[ch, there], rz_recv.at[ch, own_z], z_peers[k]))
        rz_recv[ch, own_z] = rz_send[ch, own_z]
        rz_copies.append(copies)

    recv([logit_copy])
    logits = (logit_send[...] + logit_recv[...])[:, 0:EXPERTS]
    picked0 = jnp.sum(jnp.where(pick0, logits, 0.0), axis=1, keepdims=True)
    picked1 = jnp.sum(jnp.where(pick1, logits, 0.0), axis=1, keepdims=True)
    gate0, gate1 = jax.nn.sigmoid(picked0 - picked1), jax.nn.sigmoid(picked1 - picked0)
    places = iota((TOK, SLOTS), 1).astype(F32)
    gates = jnp.where(places == from0, gate0, 0.0) + jnp.where(places == from1, gate1, 0.0)
    gates_high = gates.astype(BF16)
    gates_low = (gates - gates_high.astype(F32)).astype(BF16)

    out_copies = []
    for ch in range(CHUNKS):
        recv(rz_copies[ch])
        moe_out = dot(gates_high, rz_recv[ch]) + dot(gates_low, rz_recv[ch])
        out_send[ch] = (after[:, ch * CW : (ch + 1) * CW] + moe_out).astype(BF16)
        out_copies.append(net.send(out_send.at[ch], out_recv.at[ch], partner))
        out_ref[:, pl.ds(pl.multiple_of(s * HALF + ch * CW, CW), CW)] = out_send[ch]
    for ch in range(CHUNKS):
        recv([out_copies[ch]])
        out_ref[:, pl.ds(pl.multiple_of((1 - s) * HALF + ch * CW, CW), CW)] = out_recv[ch]
    net.finish()


def permutations():
    i = np.arange(SLOTS)
    perm = np.zeros((SLOTS, SLOTS), np.float32)
    perm[i, i % BLOCK // CAP * BLOCK + i // BLOCK * CAP + i % CAP] = 1
    perm_kv = np.zeros((TOK, TOK), np.float32)
    for kind in range(2):
        for caption in range(2):
            for p in range(32):
                row = kind * 64 + caption * 32 + p
                perm_kv[row, p // 16 * 64 + caption * 32 + p % 16 * 2 + kind] = 1
    return jnp.asarray(perm, BF16), jnp.asarray(perm_kv, BF16)


def body(
    tokens,
    memory,
    target_len,
    source_len,
    attn_gain,
    w_query,
    w_out,
    moe_gain,
    w_router,
    expert_ids,
    w_up,
    w_down,
):
    perm, perm_kv = permutations()
    vmem = pl.BlockSpec(memory_space=pltpu.VMEM)
    smem = pl.BlockSpec(memory_space=pltpu.SMEM)
    hbm = pl.BlockSpec(memory_space=pl.ANY)
    buf = lambda *shape: pltpu.VMEM(shape, BF16)
    wide = lambda *shape: pltpu.VMEM(shape, F32)
    n_sems = 128
    return pl.pallas_call(
        kernel,
        out_shape=jax.ShapeDtypeStruct((TOK, D), BF16),
        in_specs=[vmem, vmem, smem, smem] + [vmem] * 9 + [hbm, hbm],
        out_specs=vmem,
        scratch_shapes=[
            buf(8, 8, 2, 16, HALF),
            buf(8, 8, 2, 16, HALF),
            buf(D, HALF),
            buf(HALF, D),
            buf(2, 64, HALF),
            buf(TOK, HALF),
            buf(TOK, D),
            wide(TOK, HALF),
            buf(TOK, HALF),
            buf(CHUNKS, TOK, CW),
            buf(CHUNKS, TOK, CW),
            wide(TOK, HALF),
            wide(TOK, 128),
            wide(TOK, 128),
            wide(TOK, 128),
            wide(TOK, 128),
            buf(SLOTS, TOK),
            buf(CHUNKS, SLOTS, CW),
            buf(CHUNKS, SLOTS, CW),
            buf(CHUNKS, SLOTS, CW),
            buf(2, 2, CHUNKS, SLOTS, CW),
            wide(2, SLOTS, HALF),
            buf(2, SLOTS, HALF),
            buf(2 * CHUNKS, SLOTS, CW),
            buf(2 * CHUNKS, SLOTS, CW),
            buf(2 * CHUNKS, SLOTS, CW),
            buf(CHUNKS, SLOTS, CW),
            buf(CHUNKS, SLOTS, CW),
            buf(CHUNKS, SLOTS, CW),
            buf(CHUNKS, SLOTS, CW),
            buf(CHUNKS, SLOTS, CW),
            buf(CHUNKS, SLOTS, CW),
            buf(CHUNKS, TOK, CW),
            buf(CHUNKS, TOK, CW),
            pltpu.SemaphoreType.DMA((n_sems,)),
            pltpu.SemaphoreType.DMA((n_sems,)),
            pltpu.SemaphoreType.DMA((2,)),
        ],
        compiler_params=pltpu.CompilerParams(
            collective_id=0, has_side_effects=True, vmem_limit_bytes=60 << 20
        ),
        cost_estimate=pl.CostEstimate(
            flops=8_000_000_000, bytes_accessed=12_000_000, transcendentals=300_000
        ),
    )(
        tokens,
        memory.reshape(64, D),
        target_len,
        source_len,
        attn_gain.reshape(1, D),
        w_query,
        w_out.T,
        moe_gain.reshape(1, D),
        w_router,
        expert_ids,
        expert_ids.T,
        perm,
        perm_kv,
        w_up.reshape(D, HALF),
        w_down.reshape(HALF, D),
    )


def solution(mesh):
    return jax.shard_map(
        body,
        mesh=mesh,
        in_specs=(
            P("expert", None),
            P("expert", "section", None, None),
            P("expert"),
            P("expert"),
            P(),
            P("expert", "section"),
            P("section", "expert"),
            P(),
            P(),
            P("expert", None),
            P("expert", None, "section"),
            P("expert", "section", None),
        ),
        out_specs=P("expert", None),
        check_vma=False,
    )
```

```python
import functools

import jax
import jax.numpy as jnp
import numpy as np
from jax import lax
from jax.experimental import pallas as pl
from jax.experimental.pallas import tpu as pltpu
from jax.sharding import PartitionSpec as P

MESH = pl.DeviceIdType.MESH
F32 = jnp.float32
BF16 = jnp.bfloat16

HD = 128
D = 2048
HALF = 1024
TOK = 128
CAP = 6
EXPERTS = 64
SLOTS = EXPERTS * CAP
BLOCK = 8 * CAP
CHUNKS = 4
CW = HALF // CHUNKS
NZ, NY, NX = 8, 4, 2
Z_STEPS = (4, 3, 5, 2, 6, 1, 7)
EARLY = 4
EARLY_BACK = 8
PLANE = ((2, 1), (1, 1), (3, 1), (2, 0), (0, 1), (1, 0), (3, 0))


def coords():
    s = lax.axis_index("section")
    e = lax.axis_index("expert")
    return s, e // 16, (e // 4) % 4, (e // 2) % 2, e % 2


def device(s, z, y, x, c):
    return (s, ((z * NY + y) * NX + x) * 2 + c)


class Net:
    def __init__(self, send_sem, recv_sem):
        self.send_sem, self.recv_sem = send_sem, recv_sem
        self.count, self.waiting = 0, []

    def send(self, src, dst, target):
        k = self.count
        self.count += 1
        copy = pltpu.make_async_remote_copy(
            src_ref=src,
            dst_ref=dst,
            send_sem=self.send_sem.at[k],
            recv_sem=self.recv_sem.at[k],
            device_id=target,
            device_id_type=MESH,
        )
        copy.start()
        self.waiting.append(copy)
        return copy

    def sent(self, copies):
        for copy in copies:
            copy.wait_send()
            self.waiting = [other for other in self.waiting if other is not copy]

    def finish(self):
        self.sent(list(self.waiting))


def recv(copies):
    for copy in copies:
        copy.wait_recv()


def gather_z_last(net, buf, cols, forwards):
    s, z, y, x, c = coords()
    view = lambda *idx: buf.at[(*idx, slice(None), cols)]
    sibling = device(s, z, y, x, 1 - c)
    mine = view(z, y * 2 + x, c)
    a = [net.send(mine, mine, device(s, z, (y + dy) % NY, (x + dx) % NX, c)) for dy, dx in PLANE]
    yield
    recv(a)
    slab = view(z, slice(None), c)
    up, down = device(s, (z + 1) % NZ, y, x, c), device(s, (z + 7) % NZ, y, x, c)
    u, d = net.send(slab, slab, up), net.send(slab, slab, down)
    forwards.append(net.send(slab, slab, sibling))
    for step in range(1, 4):
        yield
        recv([u])
        block = view((z + 8 - step) % NZ, slice(None), c)
        part = block if step < 3 else view((z + 8 - step) % NZ, pl.ds(0, 4), c)
        u = net.send(part, part, up)
        forwards.append(net.send(block, block, sibling))
        recv([d])
        block = view((z + step) % NZ, slice(None), c)
        part = block if step < 3 else view((z + step) % NZ, pl.ds(4, 4), c)
        d = net.send(part, part, down)
        forwards.append(net.send(block, block, sibling))
    yield
    recv([u, d])
    block = view((z + 4) % NZ, slice(None), c)
    forwards.append(net.send(block, block, sibling))
    yield


def gather_y_last(net, buf, cols, forwards):
    s, z, y, x, c = coords()
    view = lambda *idx: buf.at[(*idx, slice(None), cols)]
    sibling = device(s, z, y, x, 1 - c)
    mine = view(z, y * 2 + x, c)
    a = [net.send(mine, mine, device(s, (z + d) % NZ, y, x, c)) for d in Z_STEPS]
    yield
    recv(a)
    line = view(slice(None), y * 2 + x, c)
    b = net.send(line, line, device(s, z, y, 1 - x, c))
    yield
    recv([b])
    up, down = device(s, z, (y + 1) % NY, x, c), device(s, z, (y + 3) % NY, x, c)
    slab = view(slice(None), pl.ds(y * 2, 2), c)
    u, d = net.send(slab, slab, up), net.send(slab, slab, down)
    forwards.append(net.send(slab, slab, sibling))
    yield
    recv([u])
    below = ((y + 3) % NY) * 2
    part = view(pl.ds(0, 4), pl.ds(below, 2), c)
    u = net.send(part, part, up)
    block = view(slice(None), pl.ds(below, 2), c)
    forwards.append(net.send(block, block, sibling))
    recv([d])
    above = ((y + 1) % NY) * 2
    part = view(pl.ds(4, 4), pl.ds(above, 2), c)
    d = net.send(part, part, down)
    block = view(slice(None), pl.ds(above, 2), c)
    forwards.append(net.send(block, block, sibling))
    yield
    recv([u, d])
    block = view(slice(None), pl.ds(((y + 2) % NY) * 2, 2), c)
    forwards.append(net.send(block, block, sibling))
    yield


def iota(shape, dim):
    return lax.broadcasted_iota(jnp.int32, shape, dim)


def nt_dot(a, b):
    return lax.dot_general(a, b, (((1,), (1,)), ((), ())), preferred_element_type=F32)


def dot(a, b):
    return jnp.dot(a, b, preferred_element_type=F32)


def kernel(
    tokens_hbm,
    memory_hbm,
    target_len_ref,
    source_len_ref,
    attn_gain_ref,
    w_query_hbm,
    w_out_hbm,
    moe_gain_ref,
    w_router_hbm,
    ids_t_ref,
    perm_kv_ref,
    w_up_hbm,
    w_down_hbm,
    out_ref,
    tokens_ref,
    w_router_ref,
    wq,
    wo,
    w_up,
    w_down,
    mem,
    kv,
    normed,
    query_acc,
    context,
    head_send,
    head_recv,
    after,
    stat_send,
    stat_recv,
    logit_send,
    logit_recv,
    table,
    perm_ref,
    z_send,
    z_recv,
    p_send,
    rows,
    acc,
    hidden,
    part_send,
    part_recv,
    part_own,
    rp_send,
    rp_recv,
    rz_send,
    rz_recv,
    out_send,
    out_recv,
    send_sem,
    recv_sem,
    load_sem,
):
    s, z, y, x, c = coords()
    chip = y * 2 + x
    sibling, partner = device(s, z, y, x, 1 - c), device(1 - s, z, y, x, c)
    z_peers = [device(s, (z + d) % NZ, y, x, c) for d in Z_STEPS]
    p_peers, p_chips, p_sections = [], [], []
    for ds in (1, 0):
        for dy, dx in ((0, 0), *PLANE):
            if ds or dy or dx:
                to_s, to_y, to_x = (s + ds) % 2, (y + dy) % NY, (x + dx) % NX
                p_peers.append(device(to_s, z, to_y, to_x, c))
                p_chips.append(to_y * 2 + to_x)
                p_sections.append(to_s)

    col0 = pl.multiple_of(s * HALF, HALF)
    col1 = pl.multiple_of((1 - s) * HALF, HALF)
    load_up = pltpu.make_async_copy(w_up_hbm, w_up, load_sem.at[0])
    load_down = pltpu.make_async_copy(w_down_hbm, w_down, load_sem.at[1])
    load_mem = pltpu.make_async_copy(
        memory_hbm.at[:, :, :, pl.ds(col0, HALF)], mem.at[s], load_sem.at[2]
    )
    load_tokens = pltpu.make_async_copy(tokens_hbm, tokens_ref, load_sem.at[3])
    load_router = pltpu.make_async_copy(w_router_hbm, w_router_ref, load_sem.at[4])
    load_wq = pltpu.make_async_copy(w_query_hbm, wq.at[z, chip, c], load_sem.at[5])
    load_wo = pltpu.make_async_copy(w_out_hbm, wo.at[z, chip, c], load_sem.at[6])


    def columns(k, ss):
        return pl.ds(pl.multiple_of(k * 256 + ss * 128, 128), 128)

    barrier = pltpu.get_barrier_semaphore()
    peers = [sibling, *z_peers, *p_peers]
    for peer in peers:
        pl.semaphore_signal(barrier, inc=1, device_id=peer, device_id_type=MESH)
    for load in (load_wq, load_wo, load_tokens, load_mem, load_router):
        load.start()
    load_wq.wait()
    load_wo.wait()
    pl.semaphore_wait(barrier, len(peers))

    net = Net(send_sem, recv_sem)
    left, right = pl.ds(0, HALF // 2), pl.ds(HALF // 2, HALF // 2)
    qz_forwards, qy_forwards, oz_forwards, oy_forwards = [], [], [], []
    qz = gather_z_last(net, wq, left, qz_forwards)
    qy = gather_y_last(net, wq, right, qy_forwards)
    oz = gather_z_last(net, wo, left, oz_forwards)
    oy = gather_y_last(net, wo, right, oy_forwards)
    def norm():
        load_tokens.wait()
        values = tokens_ref[...].astype(F32)
        center = values - jnp.mean(values, axis=-1, keepdims=True)
        spread = jnp.mean(center * center, axis=-1, keepdims=True)
        normed[...] = (center * lax.rsqrt(spread + 1e-05) * attn_gain_ref[...]).astype(BF16)

    from0 = from1 = pick0 = pick1 = None

    def slots():
        nonlocal from0, from1, pick0, pick1
        tl0, tl1 = target_len_ref[0], target_len_ref[1]
        t = iota((1, TOK), 1)
        live = t < jnp.where(t < 64, tl0, tl1 + 64)
        i0, i1 = ids_t_ref[0:1, :], ids_t_ref[1:2, :]
        experts = iota((EXPERTS, TOK), 0)
        hit0, hit1 = (experts == i0) & live, (experts == i1) & live
        earlier = (iota((TOK, TOK), 0) < iota((TOK, TOK), 1)).astype(F32).astype(BF16)
        before = dot((hit0.astype(F32) + hit1.astype(F32)).astype(BF16), earlier)
        slot0 = jnp.sum(jnp.where(hit0, before, 0.0), axis=0, keepdims=True)
        slot1 = jnp.sum(jnp.where(hit1, before, 0.0), axis=0, keepdims=True)
        to0 = jnp.where(live, i0.astype(F32) * CAP + slot0, -1.0)
        to1 = jnp.where(live, i1.astype(F32) * CAP + slot1, -1.0)
        places = iota((SLOTS, TOK), 0).astype(F32)
        table[...] = ((places == to0) | (places == to1)).astype(F32).astype(BF16)

        t = iota((TOK, 1), 0)
        live = t < jnp.where(t < 64, tl0, tl1 + 64)
        eye = (iota((TOK, TOK), 0) == iota((TOK, TOK), 1)).astype(F32).astype(BF16)
        ids_col = nt_dot(eye, ids_t_ref[...].astype(F32).astype(BF16))
        i0, i1 = ids_col[:, 0:1], ids_col[:, 1:2]
        experts = iota((TOK, EXPERTS), 1).astype(F32)
        pick0, pick1 = experts == i0, experts == i1
        hit0, hit1 = pick0 & live, pick1 & live
        earlier = (iota((TOK, TOK), 1) < iota((TOK, TOK), 0)).astype(F32).astype(BF16)
        before = dot(earlier, (hit0.astype(F32) + hit1.astype(F32)).astype(BF16))
        slot0 = jnp.sum(jnp.where(hit0, before, 0.0), axis=1, keepdims=True)
        slot1 = jnp.sum(jnp.where(hit1, before, 0.0), axis=1, keepdims=True)
        from0 = jnp.where(live, i0 * CAP + slot0, -1.0)
        from1 = jnp.where(live, i1 * CAP + slot1, -1.0)

        i, j = iota((SLOTS, SLOTS), 0).astype(F32), iota((SLOTS, SLOTS), 1).astype(F32)
        block = jnp.floor((i + 0.5) * (1 / BLOCK))
        inner = i - block * BLOCK
        group = jnp.floor((inner + 0.5) * (1 / CAP))
        other = group * BLOCK + block * CAP + (inner - group * CAP)
        perm_ref[...] = (j == other).astype(F32).astype(BF16)

    def keys_values():
        load_mem.wait()
        recv([mem_copy])
        kv[...] = dot(perm_kv_ref[...], mem[...].reshape(TOK, HALF)).astype(BF16)

    def add_query(side):
        query_acc[:, side] = dot(normed[...], wq[:, :, :, :, side].reshape(D, HALF // 2))

    def query_z():
        recv(qz_forwards)
        add_query(slice(0, HALF // 2))

    def query_y():
        recv(qy_forwards)
        add_query(slice(HALF // 2, HALF))

    def attention():
        sl0, sl1 = source_len_ref[0], source_len_ref[1]
        q_row, k_col = iota((TOK, 64), 0), iota((TOK, 64), 1)
        visible = (k_col >= jnp.where(q_row < 64, 0, 32)) & (
            k_col < jnp.where(q_row < 64, sl0, sl1 + 32)
        )
        for h in range(HALF // HD):
            head = slice(h * HD, (h + 1) * HD)
            query = query_acc[:, head].astype(BF16)
            scores = nt_dot(query, kv[0:64, head]) * HD ** (-0.5)
            scores = jnp.where(visible, scores, -1e30)
            scores = jnp.exp(scores - jnp.max(scores, axis=-1, keepdims=True))
            weights = (scores / jnp.sum(scores, axis=-1, keepdims=True)).astype(BF16)
            context[:, head] = dot(weights, kv[64:128, head]).astype(BF16)

    head_copies = []

    def slab(n):
        k = (z + (0, 7, 1, 6, 2, 5, 3, 4)[n]) % NZ
        if n == 0:
            recv(oy_forwards)
        recv([oz_forwards[n]])
        product = nt_dot(context[...], wo[k].reshape(256, HALF))
        mine, theirs = product[:, 0:128], product[:, 128:256]
        keep = jnp.where(s == 1, theirs, mine)
        give = jnp.where(s == 1, mine, theirs)
        head_send[k] = give.astype(BF16)
        after[k] = tokens_ref[:, columns(k, s)].astype(F32) + keep
        head_copies.append(net.send(head_send.at[k], head_recv.at[k], partner))

    mem_copy = None

    def send_memory():
        nonlocal mem_copy
        mem_copy = net.send(memory_hbm.at[:, :, :, pl.ds(col1, HALF)], mem.at[s], partner)
        load_up.start()
        load_down.start()

    next(qy)
    next(qz)
    next(oy)
    norm()
    next(qz)
    next(qy)
    next(oz)
    send_memory()
    slots()
    next(qz)
    next(qy)
    next(oy)
    next(qz)
    next(oz)
    next(oy)
    keys_values()
    next(qy)
    next(qz)
    next(oz)
    next(qy)
    next(qz)
    query_y()
    next(oz)
    next(oy)
    query_z()
    next(oz)
    attention()
    next(oy)
    next(oz)
    slab(0)
    slab(1)
    slab(2)
    slab(3)
    slab(4)
    slab(5)
    slab(6)
    slab(7)
    recv(head_copies)
    for k in range(NZ):
        after[k] += head_recv[k].astype(F32)

    values = jnp.concatenate([after[k] for k in range(NZ)], axis=1)
    mean = jnp.mean(values, axis=-1, keepdims=True)
    center = values - mean
    square = jnp.sum(center * center, axis=-1, keepdims=True)
    diagonal = iota((TOK, TOK), 0) == iota((TOK, TOK), 1)
    to_row = lambda column: jnp.sum(jnp.where(diagonal, column, 0.0), axis=0, keepdims=True)
    to_column = lambda row: jnp.sum(jnp.where(diagonal, row, 0.0), axis=1, keepdims=True)
    stat_send[...] = jnp.where(iota((8, TOK), 0) == 0, to_row(mean), to_row(square))
    stat_copy = net.send(stat_send, stat_recv, partner)
    recv([stat_copy])
    mean_other, square_other = to_column(stat_recv[0:1, :]), to_column(stat_recv[1:2, :])
    gain = jnp.concatenate([moe_gain_ref[:, columns(k, s)] for k in range(NZ)], axis=1)
    gap = mean - mean_other
    spread = (square + square_other + gap * gap * (HALF / 2)) * (1.0 / D)
    mean = (mean + mean_other) * 0.5
    moe_in = (
        (values - mean) * lax.rsqrt(spread + 1e-05) * gain
    ).astype(BF16)

    own_z = pl.ds(pl.multiple_of(z * BLOCK, 16), BLOCK)
    own_chip = pl.ds(pl.multiple_of(chip * BLOCK, 16), BLOCK)
    z_blocks = [pl.ds(pl.multiple_of((z + d) % NZ * BLOCK, 16), BLOCK) for d in Z_STEPS]
    p_blocks = [pl.ds(pl.multiple_of(there * BLOCK, 16), BLOCK) for there in p_chips]

    def send_z(ch, source, into):
        into[ch, own_z] = source[ch, own_z]
        return [
            net.send(source.at[ch, block], into.at[ch, own_z], peer)
            for block, peer in zip(z_blocks, z_peers)
        ]

    def start_z(ch):
        z_send[ch] = dot(table[...], moe_in[:, ch * CW : (ch + 1) * CW]).astype(BF16)
        return send_z(ch, z_send, z_recv)

    def add_up(cc, ch):
        pieces = [rows[cc, ch, ss, :, k * 128 : (k + 1) * 128] for k in range(2) for ss in range(2)]
        joined = jnp.concatenate(pieces, axis=1)
        for n in range(HALF // 256):
            tile = slice(n * 256, (n + 1) * 256)
            product = dot(joined, w_up[ch * 512 : (ch + 1) * 512, tile])
            if ch == 0:
                acc[cc, :, tile] = product
            else:
                acc[cc, :, tile] += product

    def finish_up(cc):
        hidden[cc] = jnp.maximum(acc[cc], 0.0).astype(BF16)

    load_up.wait()
    load_router.wait()
    z_copies, p_copies, own_forwards = [start_z(0)], [], []

    logit_send[...] = jnp.zeros_like(logit_send)
    logit_send[:, 0:EXPERTS] = nt_dot(
        moe_in, jnp.concatenate([w_router_ref[:, columns(k, s)] for k in range(NZ)], axis=1)
    )
    logit_copy = net.send(logit_send, logit_recv, partner)

    def arrived(ch):
        recv(p_copies[ch])
        mine = rows.at[c, ch]
        own_forwards.append(net.send(mine, mine, sibling))
        add_up(c, ch)

    for ch in range(CHUNKS):
        if ch + 1 < CHUNKS:
            net.sent(z_copies[ch][:EARLY])
            z_copies.append(start_z(ch + 1))
        recv(z_copies[ch])
        p_send[ch] = dot(perm_ref[...], z_recv[ch]).astype(BF16)
        rows[c, ch, s, own_chip] = p_send[ch, own_chip]
        p_copies.append(
            [
                net.send(p_send.at[ch, block], rows.at[c, ch, s, own_chip], peer)
                for block, peer in zip(p_blocks, p_peers)
            ]
        )
        if ch == CHUNKS - 1:
            arrived(1)
            recv([own_forwards[0]])
            add_up(1 - c, 0)
        elif ch == 2:
            arrived(0)
    arrived(2)
    for ch in (1, 2):
        recv([own_forwards[ch]])
        add_up(1 - c, ch)
    arrived(3)
    finish_up(c)
    recv([own_forwards[3]])
    add_up(1 - c, 3)
    finish_up(1 - c)

    load_down.wait()

    def down(cc, ch, into):
        for k in range(2):
            tile = pl.ds(ch * 512 + k * 256, 256)
            product = dot(hidden[cc], w_down[:, tile]).astype(BF16)
            into[ch, 0, :, k * 128 : (k + 1) * 128] = product[:, 0:128]
            into[ch, 1, :, k * 128 : (k + 1) * 128] = product[:, 128:256]

    def start_part(ch):
        down(1 - c, ch, part_send)
        part_copies.append(net.send(part_send.at[ch], part_recv.at[ch], sibling))

    def start_back(ch):
        recv([part_copies[ch]])
        rp_send[ch] = (part_own[ch].astype(F32) + part_recv[ch].astype(F32)).astype(BF16)
        rp_recv[ch, s, own_chip] = rp_send[ch, s, own_chip]
        return [
            net.send(rp_send.at[ch, to_s, block], rp_recv.at[ch, s, own_chip], peer)
            for to_s, block, peer in zip(p_sections, p_blocks, p_peers)
        ]

    part_copies, rp_copies, rz_copies = [], [], []
    start_part(0)
    down(c, 0, part_own)
    start_part(1)
    rp_copies.append(start_back(0))
    down(c, 1, part_own)
    start_part(2)
    down(c, 2, part_own)
    start_part(3)
    down(c, 3, part_own)

    for ch in range(CHUNKS):
        if ch + 1 < CHUNKS:
            net.sent(rp_copies[ch][:EARLY_BACK])
            rp_copies.append(start_back(ch + 1))
        recv(rp_copies[ch])
        both = dot(perm_ref[...], rp_recv[ch, 0]) + dot(perm_ref[...], rp_recv[ch, 1])
        rz_send[ch] = both.astype(BF16)
        rz_copies.append(send_z(ch, rz_send, rz_recv))

    recv([logit_copy])
    logits = (logit_send[...] + logit_recv[...])[:, 0:EXPERTS]
    picked0 = jnp.sum(jnp.where(pick0, logits, 0.0), axis=1, keepdims=True)
    picked1 = jnp.sum(jnp.where(pick1, logits, 0.0), axis=1, keepdims=True)
    gate0, gate1 = jax.nn.sigmoid(picked0 - picked1), jax.nn.sigmoid(picked1 - picked0)
    places = iota((TOK, SLOTS), 1).astype(F32)
    gates = jnp.where(places == from0, gate0, 0.0) + jnp.where(places == from1, gate1, 0.0)
    gates_high = gates.astype(BF16)
    gates_low = (gates - gates_high.astype(F32)).astype(BF16)

    out_copies = []
    for ch in range(CHUNKS):
        recv(rz_copies[ch])
        moe_out = dot(gates_high, rz_recv[ch]) + dot(gates_low, rz_recv[ch])
        kept = jnp.concatenate([after[2 * ch], after[2 * ch + 1]], axis=1)
        out_send[ch] = (kept + moe_out).astype(BF16)
        out_copies.append(net.send(out_send.at[ch], out_recv.at[ch], partner))
        for k in range(2):
            out_ref[:, columns(2 * ch + k, s)] = out_send[ch, :, k * 128 : (k + 1) * 128]
    for ch in range(CHUNKS):
        recv([out_copies[ch]])
        for k in range(2):
            out_ref[:, columns(2 * ch + k, 1 - s)] = out_recv[ch, :, k * 128 : (k + 1) * 128]
    net.finish()


def permutation_kv():
    perm_kv = np.zeros((TOK, TOK), np.float32)
    for kind in range(2):
        for caption in range(2):
            for p in range(32):
                row = kind * 64 + caption * 32 + p
                perm_kv[row, p // 16 * 64 + caption * 32 + p % 16 * 2 + kind] = 1
    return jnp.asarray(perm_kv, BF16)


def body(
    tokens,
    memory,
    target_len,
    source_len,
    attn_gain,
    w_query,
    w_out,
    moe_gain,
    w_router,
    expert_ids,
    w_up,
    w_down,
):
    perm_kv = permutation_kv()
    vmem = pl.BlockSpec(memory_space=pltpu.VMEM)
    smem = pl.BlockSpec(memory_space=pltpu.SMEM)
    hbm = pl.BlockSpec(memory_space=pl.ANY)
    buf = lambda *shape: pltpu.VMEM(shape, BF16)
    wide = lambda *shape: pltpu.VMEM(shape, F32)
    n_sems = 320
    return pl.pallas_call(
        kernel,
        out_shape=jax.ShapeDtypeStruct((TOK, D), BF16),
        in_specs=[hbm, hbm, smem, smem, vmem, hbm, hbm, vmem, hbm, vmem, vmem, hbm, hbm],
        out_specs=vmem,
        scratch_shapes=[
            buf(TOK, D),
            buf(EXPERTS, D),
            buf(8, 8, 2, 16, HALF),
            buf(8, 8, 2, 16, HALF),
            buf(D, HALF),
            buf(HALF, D),
            buf(2, 2, 16, 2, HALF),
            buf(TOK, HALF),
            buf(TOK, D),
            wide(TOK, HALF),
            buf(TOK, HALF),
            buf(NZ, TOK, 128),
            buf(NZ, TOK, 128),
            wide(NZ, TOK, 128),
            wide(8, TOK),
            wide(8, TOK),
            wide(TOK, 128),
            wide(TOK, 128),
            buf(SLOTS, TOK),
            buf(SLOTS, SLOTS),
            buf(CHUNKS, SLOTS, CW),
            buf(CHUNKS, SLOTS, CW),
            buf(CHUNKS, SLOTS, CW),
            buf(2, CHUNKS, 2, SLOTS, CW),
            wide(2, SLOTS, HALF),
            buf(2, SLOTS, HALF),
            buf(CHUNKS, 2, SLOTS, CW),
            buf(CHUNKS, 2, SLOTS, CW),
            buf(CHUNKS, 2, SLOTS, CW),
            buf(CHUNKS, 2, SLOTS, CW),
            buf(CHUNKS, 2, SLOTS, CW),
            buf(CHUNKS, SLOTS, CW),
            buf(CHUNKS, SLOTS, CW),
            buf(CHUNKS, TOK, CW),
            buf(CHUNKS, TOK, CW),
            pltpu.SemaphoreType.DMA((n_sems,)),
            pltpu.SemaphoreType.DMA((n_sems,)),
            pltpu.SemaphoreType.DMA((7,)),
        ],
        compiler_params=pltpu.CompilerParams(
            collective_id=0, has_side_effects=True, vmem_limit_bytes=60 << 20
        ),
        cost_estimate=pl.CostEstimate(
            flops=8_000_000_000, bytes_accessed=12_000_000, transcendentals=300_000
        ),
    )(
        tokens,
        memory,
        target_len,
        source_len,
        attn_gain.reshape(1, D),
        w_query,
        w_out.T,
        moe_gain.reshape(1, D),
        w_router.T,
        expert_ids.T,
        perm_kv,
        w_up.reshape(D, HALF),
        w_down.reshape(HALF, D),
    )


def solution(mesh):
    return jax.shard_map(
        body,
        mesh=mesh,
        in_specs=(
            P("expert", None),
            P("expert", "section", None, None),
            P("expert"),
            P("expert"),
            P(),
            P("expert", "section"),
            P("section", "expert"),
            P(),
            P(),
            P("expert", None),
            P("expert", None, "section"),
            P("expert", "section", None),
        ),
        out_specs=P("expert", None),
        check_vma=False,
    )
```

```python
import math

import jax
import jax.numpy as jnp
import numpy as np
from jax import lax
from jax.experimental import pallas as pl
from jax.experimental.pallas import tpu as pltpu
from jax.sharding import PartitionSpec as P

MESH = pl.DeviceIdType.MESH
F32 = jnp.float32
BF16 = jnp.bfloat16

HD = 128
D = 2048
HALF = 1024
TOK = 128
CAP = 6
EXPERTS = 64
SLOTS = EXPERTS * CAP
BLOCK = 8 * CAP
NZ, NY, NX = 8, 4, 2
O_LEFT = 384
SENDS, RECVS = 23, 79
Z_STEPS = (4, 3, 5, 2, 6, 1, 7)
DISPATCH = ((0, 1), (1, 1), (2, 2), (4, 2), (6, 1), (7, 1))
RETURN = ((0, 1), (1, 2), (3, 2), (5, 1), (6, 1), (7, 1))
PLANE = ((2, 1), (1, 1), (3, 1), (2, 0), (0, 1), (1, 0), (3, 0))


def coords():
    s = lax.axis_index("section")
    e = lax.axis_index("expert")
    return s, e // 16, (e // 4) % 4, (e // 2) % 2, e % 2


def device(s, z, y, x, c):
    return (s, ((z * NY + y) * NX + x) * 2 + c)


class Net:
    def __init__(self, send_sem, recv_sem):
        self.send_sem, self.recv_sem = send_sem, recv_sem
        self.going, self.coming = {}, {}

    def send(self, src, dst, target, out, into):
        for groups, name in ((self.going, out), (self.coming, into)):
            groups.setdefault(name, [len(groups), 0])
            groups[name][1] += math.prod(src.shape)
        pltpu.make_async_remote_copy(
            src_ref=src,
            dst_ref=dst,
            send_sem=self.send_sem.at[self.going[out][0]],
            recv_sem=self.recv_sem.at[self.coming[into][0]],
            device_id=target,
            device_id_type=MESH,
        ).start()

    def recv(self, name, like):
        k, size = self.coming[name]
        assert size == math.prod(like.shape), name
        pltpu.make_async_copy(like, like, self.recv_sem.at[k]).wait()

    def sent(self, name, like):
        k, size = self.going[name]
        assert size == math.prod(like.shape), name
        pltpu.make_async_copy(like, like, self.send_sem.at[k]).wait()


def gather_z_last(net, buf, cols, name, groups):
    s, z, y, x, c = coords()
    view = lambda *idx: buf.at[(*idx, slice(None), cols)]
    sibling = device(s, z, y, x, 1 - c)
    up, down = device(s, (z + 1) % NZ, y, x, c), device(s, (z + 7) % NZ, y, x, c)

    def forward(n, k):
        block = view(k % NZ, slice(None), c)
        net.send(block, block, sibling, name + "f", name + "f" + groups[n])

    mine = view(z, y * 2 + x, c)
    for dy, dx in PLANE:
        net.send(mine, mine, device(s, z, (y + dy) % NY, (x + dx) % NX, c), name + "p", name + "p")
    yield
    net.recv(name + "p", view(z, pl.ds(0, 7), c))
    slab = view(z, slice(None), c)
    net.send(slab, slab, up, name, name + "u0")
    net.send(slab, slab, down, name, name + "d0")
    forward(0, z)
    for step in range(1, 4):
        yield
        for way, to, k, half in (("u", up, z + 8 - step, 0), ("d", down, z + step, 4)):
            block = view(k % NZ, slice(None), c)
            net.recv(f"{name}{way}{step - 1}", block)
            part = block if step < 3 else view(k % NZ, pl.ds(half, 4), c)
            net.send(part, part, to, name, f"{name}{way}{step}")
            forward(2 * step - (way == "u"), k)
    yield
    net.recv(name + "u3", view(0, pl.ds(0, 4), c))
    net.recv(name + "d3", view(0, pl.ds(0, 4), c))
    forward(7, z + 4)
    yield


def gather_y_last(net, buf, cols, name):
    s, z, y, x, c = coords()
    view = lambda *idx: buf.at[(*idx, slice(None), cols)]
    sibling = device(s, z, y, x, 1 - c)
    up, down = device(s, z, (y + 1) % NY, x, c), device(s, z, (y + 3) % NY, x, c)
    line = lambda dy, xx, zs=slice(None): view(zs, (y + dy) % NY * 2 + xx, c)

    def forward(dy, xx):
        net.send(line(dy, xx), line(dy, xx), sibling, name + "f", name + "f")

    def first(xx, which):
        for to in (up, down):
            net.send(line(0, xx), line(0, xx), to, name, name + which)
        forward(0, xx)

    def second(xx, which):
        net.recv(name + which, view(slice(None), pl.ds(0, 2), c))
        below, above = line(3, xx, pl.ds(0, 4)), line(1, xx, pl.ds(4, 4))
        net.send(below, below, up, name, name + which + "h")
        net.send(above, above, down, name, name + which + "h")
        forward(3, xx)
        forward(1, xx)

    def last(xx, which):
        net.recv(name + which + "h", view(slice(None), 0, c))
        forward(2, xx)

    mine = view(z, y * 2 + x, c)
    for d in Z_STEPS:
        net.send(mine, mine, device(s, (z + d) % NZ, y, x, c), name + "z", name + "z")
    yield
    net.recv(name + "z", view(pl.ds(0, 7), 0, c))
    first(x, "a")
    net.send(line(0, x), line(0, x), device(s, z, y, 1 - x, c), name, name + "x")
    yield
    second(x, "a")
    yield
    net.recv(name + "x", view(slice(None), 0, c))
    first(1 - x, "b")
    yield
    second(1 - x, "b")
    yield
    last(x, "a")
    yield
    last(1 - x, "b")
    yield


def iota(shape, dim):
    return lax.broadcasted_iota(jnp.int32, shape, dim)


def nt_dot(a, b):
    return lax.dot_general(a, b, (((1,), (1,)), ((), ())), preferred_element_type=F32)


def dot(a, b):
    return jnp.dot(a, b, preferred_element_type=F32)


def kernel(
    tokens_hbm,
    memory_hbm,
    target_len_ref,
    source_len_ref,
    attn_gain_ref,
    w_query_hbm,
    w_out_hbm,
    moe_gain_ref,
    w_router_hbm,
    ids_t_ref,
    perm_kv_ref,
    w_up_hbm,
    w_down_hbm,
    out_ref,
    tokens_ref,
    w_router_ref,
    wq,
    wo,
    w_up,
    w_down,
    mem,
    kv,
    normed,
    query_acc,
    context,
    head_send,
    head_recv,
    after,
    stat_send,
    stat_recv,
    logit_send,
    logit_recv,
    table,
    perm_ref,
    z_send,
    z_recv,
    p_send,
    rows,
    acc,
    hidden,
    part_send,
    part_recv,
    part_own,
    rp_send,
    rp_recv,
    rz_send,
    rz_recv,
    out_send,
    out_recv,
    send_sem,
    recv_sem,
    load_sem,
):
    s, z, y, x, c = coords()
    chip = y * 2 + x
    sibling, partner = device(s, z, y, x, 1 - c), device(1 - s, z, y, x, c)
    z_peers = [device(s, (z + d) % NZ, y, x, c) for d in Z_STEPS]
    p_peers, p_chips, p_sections = [], [], []
    for ds in (1, 0):
        for dy, dx in ((0, 0), *PLANE):
            if ds or dy or dx:
                to_s, to_y, to_x = (s + ds) % 2, (y + dy) % NY, (x + dx) % NX
                p_peers.append(device(to_s, z, to_y, to_x, c))
                p_chips.append(to_y * 2 + to_x)
                p_sections.append(to_s)

    col0 = pl.multiple_of(s * HALF, HALF)
    col1 = pl.multiple_of((1 - s) * HALF, HALF)
    load_up = pltpu.make_async_copy(w_up_hbm, w_up, load_sem.at[0])
    load_down = pltpu.make_async_copy(w_down_hbm, w_down, load_sem.at[1])
    load_mem = pltpu.make_async_copy(
        memory_hbm.at[:, :, :, pl.ds(col0, HALF)], mem.at[s], load_sem.at[2]
    )
    load_tokens = pltpu.make_async_copy(tokens_hbm, tokens_ref, load_sem.at[3])
    load_router = pltpu.make_async_copy(w_router_hbm, w_router_ref, load_sem.at[4])
    load_wq = pltpu.make_async_copy(w_query_hbm, wq.at[z, chip, c], load_sem.at[5])
    load_wo = pltpu.make_async_copy(w_out_hbm, wo.at[z, chip, c], load_sem.at[6])


    def columns(k, ss):
        return pl.ds(pl.multiple_of(k * 256 + ss * 128, 128), 128)

    barrier = pltpu.get_barrier_semaphore()
    peers = [sibling, *z_peers, *p_peers]
    for peer in peers:
        pl.semaphore_signal(barrier, inc=1, device_id=peer, device_id_type=MESH)
    for load in (load_wq, load_wo, load_tokens, load_mem, load_router):
        load.start()
    load_wq.wait()
    load_wo.wait()
    pl.semaphore_wait(barrier, len(peers))

    net = Net(send_sem, recv_sem)
    left, right = pl.ds(0, HALF // 2), pl.ds(HALF // 2, HALF // 2)
    less, more = pl.ds(0, O_LEFT), pl.ds(O_LEFT, HALF - O_LEFT)
    qz = gather_z_last(net, wq, left, "qz", [""] * NZ)
    qy = gather_y_last(net, wq, right, "qy")
    oz = gather_z_last(net, wo, less, "oz", ["0", "1", "1", "3", "3", "5", "5", "7"])
    oy = gather_y_last(net, wo, more, "oy")

    def norm():
        load_tokens.wait()
        values = tokens_ref[...].astype(F32)
        center = values - jnp.mean(values, axis=-1, keepdims=True)
        spread = jnp.mean(center * center, axis=-1, keepdims=True)
        normed[...] = (center * lax.rsqrt(spread + 1e-05) * attn_gain_ref[...]).astype(BF16)

    from0 = from1 = pick0 = pick1 = None

    def slots():
        nonlocal from0, from1, pick0, pick1
        tl0, tl1 = target_len_ref[0], target_len_ref[1]
        t = iota((1, TOK), 1)
        live = t < jnp.where(t < 64, tl0, tl1 + 64)
        i0, i1 = ids_t_ref[0:1, :], ids_t_ref[1:2, :]
        experts = iota((EXPERTS, TOK), 0)
        hit0, hit1 = (experts == i0) & live, (experts == i1) & live
        earlier = (iota((TOK, TOK), 0) < iota((TOK, TOK), 1)).astype(F32).astype(BF16)
        before = dot((hit0.astype(F32) + hit1.astype(F32)).astype(BF16), earlier)
        slot0 = jnp.sum(jnp.where(hit0, before, 0.0), axis=0, keepdims=True)
        slot1 = jnp.sum(jnp.where(hit1, before, 0.0), axis=0, keepdims=True)
        to0 = jnp.where(live, i0.astype(F32) * CAP + slot0, -1.0)
        to1 = jnp.where(live, i1.astype(F32) * CAP + slot1, -1.0)
        places = iota((SLOTS, TOK), 0).astype(F32)
        table[...] = ((places == to0) | (places == to1)).astype(F32).astype(BF16)

        t = iota((TOK, 1), 0)
        live = t < jnp.where(t < 64, tl0, tl1 + 64)
        eye = (iota((TOK, TOK), 0) == iota((TOK, TOK), 1)).astype(F32).astype(BF16)
        ids_col = nt_dot(eye, ids_t_ref[...].astype(F32).astype(BF16))
        i0, i1 = ids_col[:, 0:1], ids_col[:, 1:2]
        experts = iota((TOK, EXPERTS), 1).astype(F32)
        pick0, pick1 = experts == i0, experts == i1
        hit0, hit1 = pick0 & live, pick1 & live
        earlier = (iota((TOK, TOK), 1) < iota((TOK, TOK), 0)).astype(F32).astype(BF16)
        before = dot(earlier, (hit0.astype(F32) + hit1.astype(F32)).astype(BF16))
        slot0 = jnp.sum(jnp.where(hit0, before, 0.0), axis=1, keepdims=True)
        slot1 = jnp.sum(jnp.where(hit1, before, 0.0), axis=1, keepdims=True)
        from0 = jnp.where(live, i0 * CAP + slot0, -1.0)
        from1 = jnp.where(live, i1 * CAP + slot1, -1.0)

        i, j = iota((SLOTS, SLOTS), 0).astype(F32), iota((SLOTS, SLOTS), 1).astype(F32)
        block = jnp.floor((i + 0.5) * (1 / BLOCK))
        inner = i - block * BLOCK
        group = jnp.floor((inner + 0.5) * (1 / CAP))
        other = group * BLOCK + block * CAP + (inner - group * CAP)
        perm_ref[...] = (j == other).astype(F32).astype(BF16)

    def keys_values():
        load_mem.wait()
        net.recv("memory", mem.at[0])
        kv[...] = dot(perm_kv_ref[...], mem[...].reshape(TOK, HALF)).astype(BF16)

    def add_query(side):
        query_acc[:, side] = dot(normed[...], wq[:, :, :, :, side].reshape(D, HALF // 2))

    def query_z():
        net.recv("qzf", wq.at[:, :, 1 - c, :, left])
        add_query(slice(0, HALF // 2))

    def query_y():
        net.recv("qyf", wq.at[:, :, 1 - c, :, right])
        add_query(slice(HALF // 2, HALF))

    def attention():
        sl0, sl1 = source_len_ref[0], source_len_ref[1]
        q_row, k_col = iota((TOK, 64), 0), iota((TOK, 64), 1)
        visible = (k_col >= jnp.where(q_row < 64, 0, 32)) & (
            k_col < jnp.where(q_row < 64, sl0, sl1 + 32)
        )
        for h in range(HALF // HD):
            head = slice(h * HD, (h + 1) * HD)
            query = query_acc[:, head].astype(BF16)
            scores = nt_dot(query, kv[0:64, head]) * HD ** (-0.5)
            scores = jnp.where(visible, scores, -1e30)
            scores = jnp.exp(scores - jnp.max(scores, axis=-1, keepdims=True))
            weights = (scores / jnp.sum(scores, axis=-1, keepdims=True)).astype(BF16)
            context[:, head] = dot(weights, kv[64:128, head]).astype(BF16)

    def project(*ns):
        if 0 in ns:
            net.recv("oyf", wo.at[:, :, 1 - c, :, more])
        net.recv(f"ozf{ns[0]}", wo.at[pl.ds(0, len(ns)), :, 1 - c, :, less])
        ks = [(z + (0, 7, 1, 6, 2, 5, 3, 4)[n]) % NZ for n in ns]
        products = [nt_dot(context[...], wo[k].reshape(256, HALF)) for k in ks]
        for k, product in zip(ks, products):
            mine, theirs = product[:, 0:128], product[:, 128:256]
            head_send[k] = jnp.where(s == 1, mine, theirs).astype(BF16)
            after[k] = tokens_ref[:, columns(k, s)].astype(F32) + jnp.where(s == 1, theirs, mine)
        for k in ks:
            net.send(head_send.at[k], head_recv.at[k], partner, "head", "head")

    def send_memory():
        theirs = memory_hbm.at[:, :, :, pl.ds(col1, HALF)]
        net.send(theirs, mem.at[s], partner, "memory", "memory")
        load_up.start()
        load_down.start()

    next(qy)
    next(qz)
    next(oy)
    next(oz)
    norm()
    next(qz)
    next(qy)
    slots()
    next(oy)
    next(qz)
    next(oz)
    next(qy)
    next(qy)
    next(oy)
    next(oy)
    send_memory()
    next(qz)
    next(oz)
    next(qy)
    next(qy)
    next(qz)
    next(qy)
    next(oy)
    next(oy)
    next(oz)
    next(qz)
    keys_values()
    query_y()
    query_z()
    attention()
    next(oz)
    next(oy)
    project(0)
    project(1, 2)
    project(3, 4)
    project(5, 6)
    next(oz)
    project(7)
    net.recv("head", head_recv)
    for k in range(NZ):
        after[k] += head_recv[k].astype(F32)

    values = jnp.concatenate([after[k] for k in range(NZ)], axis=1)
    mean = jnp.mean(values, axis=-1, keepdims=True)
    center = values - mean
    square = jnp.sum(center * center, axis=-1, keepdims=True)
    diagonal = iota((TOK, TOK), 0) == iota((TOK, TOK), 1)
    to_row = lambda column: jnp.sum(jnp.where(diagonal, column, 0.0), axis=0, keepdims=True)
    to_column = lambda row: jnp.sum(jnp.where(diagonal, row, 0.0), axis=1, keepdims=True)
    stat_send[...] = jnp.where(iota((8, TOK), 0) == 0, to_row(mean), to_row(square))
    net.send(stat_send, stat_recv, partner, "stat", "stat")
    net.recv("stat", stat_recv)
    mean_other, square_other = to_column(stat_recv[0:1, :]), to_column(stat_recv[1:2, :])
    gain = jnp.concatenate([moe_gain_ref[:, columns(k, s)] for k in range(NZ)], axis=1)
    gap = mean - mean_other
    spread = (square + square_other + gap * gap * (HALF / 2)) * (1.0 / D)
    mean = (mean + mean_other) * 0.5
    moe_in = (
        (values - mean) * lax.rsqrt(spread + 1e-05) * gain
    ).astype(BF16)

    own_z = pl.ds(pl.multiple_of(z * BLOCK, 16), BLOCK)
    own_chip = pl.ds(pl.multiple_of(chip * BLOCK, 16), BLOCK)
    z_blocks = [pl.ds(pl.multiple_of((z + d) % NZ * BLOCK, 16), BLOCK) for d in Z_STEPS]
    p_blocks = [pl.ds(pl.multiple_of(there * BLOCK, 16), BLOCK) for there in p_chips]

    def span(chunk):
        return pl.ds(chunk[0], chunk[1])

    def slabs(chunk):
        return range(chunk[0], chunk[0] + chunk[1])

    def side_by_side(parts):
        return jnp.concatenate(list(parts), axis=1)

    def spread(into, chunk, wide):
        for n, k in enumerate(slabs(chunk)):
            into[k] = wide[:, n * 128 : (n + 1) * 128].astype(into.dtype)

    def send_z(ch, chunk, source, into, name):
        into[span(chunk), own_z] = source[span(chunk), own_z]
        for block, peer in zip(z_blocks, z_peers):
            net.send(source.at[span(chunk), block], into.at[span(chunk), own_z], peer, name, f"{name}{ch}")

    def start_z(ch):
        chunk = DISPATCH[ch]
        columns_of = slice(chunk[0] * 128, (chunk[0] + chunk[1]) * 128)
        spread(z_send, chunk, dot(table[...], moe_in[:, columns_of]))
        send_z(ch, chunk, z_send, z_recv, "z")

    def add_up(cc, chunk):
        joined = side_by_side(rows[cc, k, ss] for k in slabs(chunk) for ss in range(2))
        depth = slice(chunk[0] * 256, (chunk[0] + chunk[1]) * 256)
        for n in range(HALF // 256):
            tile = slice(n * 256, (n + 1) * 256)
            product = dot(joined, w_up[depth, tile])
            if chunk[0] == 0:
                acc[cc, :, tile] = product
            else:
                acc[cc, :, tile] += product

    def finish_up(cc):
        hidden[cc] = jnp.maximum(acc[cc], 0.0).astype(BF16)

    load_up.wait()
    load_router.wait()
    for ch in range(len(DISPATCH)):
        start_z(ch)

    logit_send[...] = jnp.zeros_like(logit_send)
    logit_send[:, 0:EXPERTS] = nt_dot(
        moe_in, jnp.concatenate([w_router_ref[:, columns(k, s)] for k in range(NZ)], axis=1)
    )
    net.send(logit_send, logit_recv, partner, "logit", "logit")

    def like_plane(chunk):
        return z_recv.at[pl.ds(0, 5), pl.ds(0, 3 * BLOCK * chunk[1])]

    def arrived(ch):
        chunk = DISPATCH[ch]
        net.recv(f"p{ch}", like_plane(chunk))
        mine = rows.at[c, span(chunk)]
        net.send(mine, mine, sibling, "f", f"f{ch}")
        add_up(c, chunk)

    def passed_on(ch):
        net.recv(f"f{ch}", rows.at[1 - c, span(DISPATCH[ch])])
        add_up(1 - c, DISPATCH[ch])

    last = len(DISPATCH) - 1
    for ch, chunk in enumerate(DISPATCH):
        net.recv(f"z{ch}", z_recv.at[span(chunk), pl.ds(0, 7 * BLOCK)])
        spread(p_send, chunk, dot(perm_ref[...], side_by_side(z_recv[k] for k in slabs(chunk))))
        rows[c, span(chunk), s, own_chip] = p_send[span(chunk), own_chip]
        for block, peer in zip(p_blocks, p_peers):
            there = rows.at[c, span(chunk), s, own_chip]
            net.send(p_send.at[span(chunk), block], there, peer, "p", f"p{ch}")
        if ch >= 2:
            arrived(ch - 2)
        if ch >= 3:
            passed_on(ch - 3)
    arrived(last - 1)
    passed_on(last - 2)
    passed_on(last - 1)
    arrived(last)
    finish_up(c)
    passed_on(last)
    finish_up(1 - c)

    load_down.wait()

    def down(cc, ch, into):
        for k in slabs(RETURN[ch]):
            product = dot(hidden[cc], w_down[:, k * 256 : (k + 1) * 256]).astype(BF16)
            into[k, 0] = product[:, 0:128]
            into[k, 1] = product[:, 128:256]

    def give_part(ch):
        where = span(RETURN[ch])
        down(1 - c, ch, part_send)
        net.send(part_send.at[where], part_recv.at[where], sibling, "part", f"part{ch}")

    def start_back(ch):
        where = span(RETURN[ch])
        net.recv(f"part{ch}", part_recv.at[where])
        rp_send[where] = (part_own[where].astype(F32) + part_recv[where].astype(F32)).astype(BF16)
        rp_recv[where, s, own_chip] = rp_send[where, s, own_chip]
        for to_s, block, peer in zip(p_sections, p_blocks, p_peers):
            there = rp_recv.at[where, s, own_chip]
            net.send(rp_send.at[where, to_s, block], there, peer, "rp", f"rp{ch}")

    give_part(0)
    down(c, 0, part_own)
    for ch in range(len(RETURN)):
        if ch + 1 < len(RETURN):
            give_part(ch + 1)
        start_back(ch)
        if ch + 1 < len(RETURN):
            down(c, ch + 1, part_own)

    for ch, chunk in enumerate(RETURN):
        net.recv(f"rp{ch}", like_plane(chunk))
        both = [dot(perm_ref[...], side_by_side(rp_recv[k, ss] for k in slabs(chunk))) for ss in range(2)]
        spread(rz_send, chunk, both[0] + both[1])
        send_z(ch, chunk, rz_send, rz_recv, "rz")

    net.recv("logit", logit_recv)
    logits = (logit_send[...] + logit_recv[...])[:, 0:EXPERTS]
    picked0 = jnp.sum(jnp.where(pick0, logits, 0.0), axis=1, keepdims=True)
    picked1 = jnp.sum(jnp.where(pick1, logits, 0.0), axis=1, keepdims=True)
    gate0, gate1 = jax.nn.sigmoid(picked0 - picked1), jax.nn.sigmoid(picked1 - picked0)
    places = iota((TOK, SLOTS), 1).astype(F32)
    gates = jnp.where(places == from0, gate0, 0.0) + jnp.where(places == from1, gate1, 0.0)
    gates_high = gates.astype(BF16)
    gates_low = (gates - gates_high.astype(F32)).astype(BF16)

    for ch, chunk in enumerate(RETURN):
        net.recv(f"rz{ch}", rz_recv.at[span(chunk), pl.ds(0, 7 * BLOCK)])
        returned = side_by_side(rz_recv[k] for k in slabs(chunk))
        moe_out = dot(gates_high, returned) + dot(gates_low, returned)
        spread(out_send, chunk, side_by_side(after[k] for k in slabs(chunk)) + moe_out)
        net.send(out_send.at[span(chunk)], out_recv.at[span(chunk)], partner, "out", "out")
        for k in slabs(chunk):
            out_ref[:, columns(k, s)] = out_send[k]
    net.recv("out", out_recv)
    for k in range(NZ):
        out_ref[:, columns(k, 1 - s)] = out_recv[k]
    like_planes = rows.at[:, pl.ds(0, 5), :, pl.ds(0, 6 * BLOCK)]
    for name, like in (
        ("memory", mem.at[0]),
        ("head", head_send),
        ("stat", stat_send),
        ("logit", logit_send),
        ("z", z_send.at[:, pl.ds(0, 7 * BLOCK)]),
        ("p", like_planes),
        ("f", rows.at[c]),
        ("part", part_send),
        ("rp", like_planes),
        ("rz", rz_send.at[:, pl.ds(0, 7 * BLOCK)]),
        ("out", out_send),
    ):
        net.sent(name, like)
    for name, buf, cols in (("qz", wq, left), ("oz", wo, less)):
        net.sent(name + "p", buf.at[0, pl.ds(0, 7), c, :, cols])
        net.sent(name, buf.at[pl.ds(0, 7), :, c, :, cols])
        net.sent(name + "f", buf.at[:, :, c, :, cols])
    for name, buf, cols in (("qy", wq, right), ("oy", wo, more)):
        net.sent(name + "z", buf.at[pl.ds(0, 7), 0, c, :, cols])
        net.sent(name, buf.at[:, pl.ds(0, 7), c, :, cols])
        net.sent(name + "f", buf.at[:, :, c, :, cols])
    assert len(net.going) <= SENDS and len(net.coming) <= RECVS, (len(net.going), len(net.coming))


def permutation_kv():
    perm_kv = np.zeros((TOK, TOK), np.float32)
    for kind in range(2):
        for caption in range(2):
            for p in range(32):
                row = kind * 64 + caption * 32 + p
                perm_kv[row, p // 16 * 64 + caption * 32 + p % 16 * 2 + kind] = 1
    return jnp.asarray(perm_kv, BF16)


def body(
    tokens,
    memory,
    target_len,
    source_len,
    attn_gain,
    w_query,
    w_out,
    moe_gain,
    w_router,
    expert_ids,
    w_up,
    w_down,
):
    perm_kv = permutation_kv()
    vmem = pl.BlockSpec(memory_space=pltpu.VMEM)
    smem = pl.BlockSpec(memory_space=pltpu.SMEM)
    hbm = pl.BlockSpec(memory_space=pl.ANY)
    buf = lambda *shape: pltpu.VMEM(shape, BF16)
    wide = lambda *shape: pltpu.VMEM(shape, F32)
    return pl.pallas_call(
        kernel,
        out_shape=jax.ShapeDtypeStruct((TOK, D), BF16),
        in_specs=[hbm, hbm, smem, smem, vmem, hbm, hbm, vmem, hbm, vmem, vmem, hbm, hbm],
        out_specs=vmem,
        scratch_shapes=[
            buf(TOK, D),
            buf(EXPERTS, D),
            buf(8, 8, 2, 16, HALF),
            buf(8, 8, 2, 16, HALF),
            buf(D, HALF),
            buf(HALF, D),
            buf(2, 2, 16, 2, HALF),
            buf(TOK, HALF),
            buf(TOK, D),
            wide(TOK, HALF),
            buf(TOK, HALF),
            buf(NZ, TOK, 128),
            buf(NZ, TOK, 128),
            wide(NZ, TOK, 128),
            wide(8, TOK),
            wide(8, TOK),
            wide(TOK, 128),
            wide(TOK, 128),
            buf(SLOTS, TOK),
            buf(SLOTS, SLOTS),
            buf(NZ, SLOTS, 128),
            buf(NZ, SLOTS, 128),
            buf(NZ, SLOTS, 128),
            buf(2, NZ, 2, SLOTS, 128),
            wide(2, SLOTS, HALF),
            buf(2, SLOTS, HALF),
            buf(NZ, 2, SLOTS, 128),
            buf(NZ, 2, SLOTS, 128),
            buf(NZ, 2, SLOTS, 128),
            buf(NZ, 2, SLOTS, 128),
            buf(NZ, 2, SLOTS, 128),
            buf(NZ, SLOTS, 128),
            buf(NZ, SLOTS, 128),
            buf(NZ, TOK, 128),
            buf(NZ, TOK, 128),
            pltpu.SemaphoreType.DMA((SENDS,)),
            pltpu.SemaphoreType.DMA((RECVS,)),
            pltpu.SemaphoreType.DMA((7,)),
        ],
        compiler_params=pltpu.CompilerParams(
            collective_id=0, has_side_effects=True, vmem_limit_bytes=60 << 20
        ),
        cost_estimate=pl.CostEstimate(
            flops=8_000_000_000, bytes_accessed=12_000_000, transcendentals=300_000
        ),
    )(
        tokens,
        memory,
        target_len,
        source_len,
        attn_gain.reshape(1, D),
        w_query,
        w_out.T,
        moe_gain.reshape(1, D),
        w_router.T,
        expert_ids.T,
        perm_kv,
        w_up.reshape(D, HALF),
        w_down.reshape(HALF, D),
    )


def solution(mesh):
    return jax.shard_map(
        body,
        mesh=mesh,
        in_specs=(
            P("expert", None),
            P("expert", "section", None, None),
            P("expert"),
            P("expert"),
            P(),
            P("expert", "section"),
            P("section", "expert"),
            P(),
            P(),
            P("expert", None),
            P("expert", None, "section"),
            P("expert", "section", None),
        ),
        out_specs=P("expert", None),
        check_vma=False,
    )
```

```python
import math

import jax
import jax.numpy as jnp
import numpy as np
from jax import lax
from jax.experimental import pallas as pl
from jax.experimental.pallas import tpu as pltpu
from jax.sharding import PartitionSpec as P

MESH = pl.DeviceIdType.MESH
F32 = jnp.float32
BF16 = jnp.bfloat16

HD = 128
D = 2048
HALF = 1024
TOK = 128
CAP = 6
EXPERTS = 64
SLOTS = EXPERTS * CAP
BLOCK = 8 * CAP
NZ, NY, NX = 8, 4, 2
O_LEFT = 512
SENDS, RECVS = 23, 88
Z_STEPS = (4, 3, 5, 2, 6, 1, 7)
DISPATCH = ((0, 1), (1, 1), (2, 1), (3, 1), (4, 2), (6, 1), (7, 1))
RETURN = ((0, 1), (1, 1), (2, 1), (3, 1), (4, 1), (5, 1), (6, 1), (7, 1))
PLANE = ((2, 1), (1, 1), (3, 1), (2, 0), (0, 1), (1, 0), (3, 0))


def coords():
    s = lax.axis_index("section")
    e = lax.axis_index("expert")
    return s, e // 16, (e // 4) % 4, (e // 2) % 2, e % 2


def device(s, z, y, x, c):
    return (s, ((z * NY + y) * NX + x) * 2 + c)


class Net:
    def __init__(self, send_sem, recv_sem):
        self.send_sem, self.recv_sem = send_sem, recv_sem
        self.going, self.coming = {}, {}

    def send(self, src, dst, target, out, into):
        for groups, name in ((self.going, out), (self.coming, into)):
            groups.setdefault(name, [len(groups), 0])
            groups[name][1] += math.prod(src.shape)
        pltpu.make_async_remote_copy(
            src_ref=src,
            dst_ref=dst,
            send_sem=self.send_sem.at[self.going[out][0]],
            recv_sem=self.recv_sem.at[self.coming[into][0]],
            device_id=target,
            device_id_type=MESH,
        ).start()

    def recv(self, name, like):
        k, size = self.coming[name]
        assert size == math.prod(like.shape), name
        pltpu.make_async_copy(like, like, self.recv_sem.at[k]).wait()

    def sent(self, name, like):
        k, size = self.going[name]
        assert size == math.prod(like.shape), name
        pltpu.make_async_copy(like, like, self.send_sem.at[k]).wait()


def gather_z_last(net, buf, cols, name, groups):
    s, z, y, x, c = coords()
    view = lambda *idx: buf.at[(*idx, slice(None), cols)]
    sibling = device(s, z, y, x, 1 - c)
    up, down = device(s, (z + 1) % NZ, y, x, c), device(s, (z + 7) % NZ, y, x, c)

    def forward(n, k):
        block = view(k % NZ, slice(None), c)
        net.send(block, block, sibling, name + "f", name + "f" + groups[n])

    mine = view(z, y * 2 + x, c)
    for dy, dx in PLANE:
        net.send(mine, mine, device(s, z, (y + dy) % NY, (x + dx) % NX, c), name + "p", name + "p")
    yield
    net.recv(name + "p", view(z, pl.ds(0, 7), c))
    slab = view(z, slice(None), c)
    net.send(slab, slab, up, name, name + "u0")
    net.send(slab, slab, down, name, name + "d0")
    forward(0, z)
    for step in range(1, 4):
        yield
        for way, to, k, half in (("u", up, z + 8 - step, 0), ("d", down, z + step, 4)):
            block = view(k % NZ, slice(None), c)
            net.recv(f"{name}{way}{step - 1}", block)
            part = block if step < 3 else view(k % NZ, pl.ds(half, 4), c)
            net.send(part, part, to, name, f"{name}{way}{step}")
            forward(2 * step - (way == "u"), k)
    yield
    net.recv(name + "u3", view(0, pl.ds(0, 4), c))
    net.recv(name + "d3", view(0, pl.ds(0, 4), c))
    forward(7, z + 4)
    yield


def gather_y_last(net, buf, cols, name):
    s, z, y, x, c = coords()
    view = lambda *idx: buf.at[(*idx, slice(None), cols)]
    sibling = device(s, z, y, x, 1 - c)
    up, down = device(s, z, (y + 1) % NY, x, c), device(s, z, (y + 3) % NY, x, c)
    line = lambda dy, xx, zs=slice(None): view(zs, (y + dy) % NY * 2 + xx, c)

    def forward(dy, xx):
        net.send(line(dy, xx), line(dy, xx), sibling, name + "f", name + "f")

    def first(xx, which):
        for to in (up, down):
            net.send(line(0, xx), line(0, xx), to, name, name + which)
        forward(0, xx)

    def second(xx, which):
        net.recv(name + which, view(slice(None), pl.ds(0, 2), c))
        below, above = line(3, xx, pl.ds(0, 4)), line(1, xx, pl.ds(4, 4))
        net.send(below, below, up, name, name + which + "h")
        net.send(above, above, down, name, name + which + "h")
        forward(3, xx)
        forward(1, xx)

    def last(xx, which):
        net.recv(name + which + "h", view(slice(None), 0, c))
        forward(2, xx)

    mine = view(z, y * 2 + x, c)
    for d in Z_STEPS:
        net.send(mine, mine, device(s, (z + d) % NZ, y, x, c), name + "z", name + "z")
    yield
    net.recv(name + "z", view(pl.ds(0, 7), 0, c))
    first(x, "a")
    net.send(line(0, x), line(0, x), device(s, z, y, 1 - x, c), name, name + "x")
    yield
    second(x, "a")
    yield
    net.recv(name + "x", view(slice(None), 0, c))
    first(1 - x, "b")
    yield
    second(1 - x, "b")
    yield
    last(x, "a")
    yield
    last(1 - x, "b")
    yield


def iota(shape, dim):
    return lax.broadcasted_iota(jnp.int32, shape, dim)


def nt_dot(a, b):
    return lax.dot_general(a, b, (((1,), (1,)), ((), ())), preferred_element_type=F32)


def dot(a, b):
    return jnp.dot(a, b, preferred_element_type=F32)


def kernel(
    tokens_hbm,
    memory_hbm,
    target_len_ref,
    source_len_ref,
    attn_gain_ref,
    w_query_hbm,
    w_out_hbm,
    moe_gain_ref,
    w_router_hbm,
    ids_t_ref,
    perm_kv_ref,
    w_up_hbm,
    w_down_hbm,
    out_ref,
    tokens_ref,
    w_router_ref,
    wq,
    wo,
    w_up,
    w_down,
    mem,
    kv,
    normed,
    query_acc,
    context,
    head_send,
    head_recv,
    after,
    stat_send,
    stat_recv,
    logit_send,
    logit_recv,
    table,
    perm_ref,
    z_send,
    z_recv,
    p_send,
    rows,
    acc,
    hidden,
    part_send,
    part_recv,
    part_own,
    rp_send,
    rp_recv,
    rz_send,
    rz_recv,
    out_send,
    out_recv,
    send_sem,
    recv_sem,
    load_sem,
):
    s, z, y, x, c = coords()
    chip = y * 2 + x
    sibling, partner = device(s, z, y, x, 1 - c), device(1 - s, z, y, x, c)
    z_peers = [device(s, (z + d) % NZ, y, x, c) for d in Z_STEPS]
    p_peers, p_chips, p_sections = [], [], []
    for ds in (1, 0):
        for dy, dx in ((0, 0), *PLANE):
            if ds or dy or dx:
                to_s, to_y, to_x = (s + ds) % 2, (y + dy) % NY, (x + dx) % NX
                p_peers.append(device(to_s, z, to_y, to_x, c))
                p_chips.append(to_y * 2 + to_x)
                p_sections.append(to_s)

    col0 = pl.multiple_of(s * HALF, HALF)
    col1 = pl.multiple_of((1 - s) * HALF, HALF)
    load_up = pltpu.make_async_copy(w_up_hbm, w_up, load_sem.at[0])
    load_down = pltpu.make_async_copy(w_down_hbm, w_down, load_sem.at[1])
    load_mem = pltpu.make_async_copy(
        memory_hbm.at[:, :, :, pl.ds(col0, HALF)], mem.at[s], load_sem.at[2]
    )
    load_tokens = pltpu.make_async_copy(tokens_hbm, tokens_ref, load_sem.at[3])
    load_router = pltpu.make_async_copy(w_router_hbm, w_router_ref, load_sem.at[4])
    load_wq = pltpu.make_async_copy(w_query_hbm, wq.at[z, chip, c], load_sem.at[5])
    load_wo = pltpu.make_async_copy(w_out_hbm, wo.at[z, chip, c], load_sem.at[6])


    def columns(k, ss):
        return pl.ds(pl.multiple_of(k * 256 + ss * 128, 128), 128)

    barrier = pltpu.get_barrier_semaphore()
    peers = [sibling, *z_peers, *p_peers]
    for peer in peers:
        pl.semaphore_signal(barrier, inc=1, device_id=peer, device_id_type=MESH)
    for load in (load_wq, load_wo, load_tokens, load_mem, load_router):
        load.start()
    load_wq.wait()
    load_wo.wait()
    pl.semaphore_wait(barrier, len(peers))

    net = Net(send_sem, recv_sem)
    left, right = pl.ds(0, HALF // 2), pl.ds(HALF // 2, HALF // 2)
    less, more = pl.ds(0, O_LEFT), pl.ds(O_LEFT, HALF - O_LEFT)
    qz = gather_z_last(net, wq, left, "qz", [""] * NZ)
    qy = gather_y_last(net, wq, right, "qy")
    oz = gather_z_last(net, wo, less, "oz", ["0", "1", "1", "3", "3", "5", "5", "7"])
    oy = gather_y_last(net, wo, more, "oy")

    def norm():
        load_tokens.wait()
        values = tokens_ref[...].astype(F32)
        center = values - jnp.mean(values, axis=-1, keepdims=True)
        spread = jnp.mean(center * center, axis=-1, keepdims=True)
        normed[...] = (center * lax.rsqrt(spread + 1e-05) * attn_gain_ref[...]).astype(BF16)

    from0 = from1 = pick0 = pick1 = None

    def slots():
        nonlocal from0, from1, pick0, pick1
        tl0, tl1 = target_len_ref[0], target_len_ref[1]
        t = iota((1, TOK), 1)
        live = t < jnp.where(t < 64, tl0, tl1 + 64)
        i0, i1 = ids_t_ref[0:1, :], ids_t_ref[1:2, :]
        experts = iota((EXPERTS, TOK), 0)
        hit0, hit1 = (experts == i0) & live, (experts == i1) & live
        earlier = (iota((TOK, TOK), 0) < iota((TOK, TOK), 1)).astype(F32).astype(BF16)
        before = dot((hit0.astype(F32) + hit1.astype(F32)).astype(BF16), earlier)
        slot0 = jnp.sum(jnp.where(hit0, before, 0.0), axis=0, keepdims=True)
        slot1 = jnp.sum(jnp.where(hit1, before, 0.0), axis=0, keepdims=True)
        to0 = jnp.where(live, i0.astype(F32) * CAP + slot0, -1.0)
        to1 = jnp.where(live, i1.astype(F32) * CAP + slot1, -1.0)
        places = iota((SLOTS, TOK), 0).astype(F32)
        table[...] = ((places == to0) | (places == to1)).astype(F32).astype(BF16)

        t = iota((TOK, 1), 0)
        live = t < jnp.where(t < 64, tl0, tl1 + 64)
        eye = (iota((TOK, TOK), 0) == iota((TOK, TOK), 1)).astype(F32).astype(BF16)
        ids_col = nt_dot(eye, ids_t_ref[...].astype(F32).astype(BF16))
        i0, i1 = ids_col[:, 0:1], ids_col[:, 1:2]
        experts = iota((TOK, EXPERTS), 1).astype(F32)
        pick0, pick1 = experts == i0, experts == i1
        hit0, hit1 = pick0 & live, pick1 & live
        earlier = (iota((TOK, TOK), 1) < iota((TOK, TOK), 0)).astype(F32).astype(BF16)
        before = dot(earlier, (hit0.astype(F32) + hit1.astype(F32)).astype(BF16))
        slot0 = jnp.sum(jnp.where(hit0, before, 0.0), axis=1, keepdims=True)
        slot1 = jnp.sum(jnp.where(hit1, before, 0.0), axis=1, keepdims=True)
        from0 = jnp.where(live, i0 * CAP + slot0, -1.0)
        from1 = jnp.where(live, i1 * CAP + slot1, -1.0)

        i, j = iota((SLOTS, SLOTS), 0).astype(F32), iota((SLOTS, SLOTS), 1).astype(F32)
        block = jnp.floor((i + 0.5) * (1 / BLOCK))
        inner = i - block * BLOCK
        group = jnp.floor((inner + 0.5) * (1 / CAP))
        other = group * BLOCK + block * CAP + (inner - group * CAP)
        perm_ref[...] = (j == other).astype(F32).astype(BF16)

    def keys_values():
        load_mem.wait()
        net.recv("memory", mem.at[0])
        kv[...] = dot(perm_kv_ref[...], mem[...].reshape(TOK, HALF)).astype(BF16)

    def add_query(side):
        query_acc[:, side] = dot(normed[...], wq[:, :, :, :, side].reshape(D, HALF // 2))

    def query_z():
        net.recv("qzf", wq.at[:, :, 1 - c, :, left])
        add_query(slice(0, HALF // 2))

    def query_y():
        net.recv("qyf", wq.at[:, :, 1 - c, :, right])
        add_query(slice(HALF // 2, HALF))

    def attention():
        sl0, sl1 = source_len_ref[0], source_len_ref[1]
        q_row, k_col = iota((TOK, 64), 0), iota((TOK, 64), 1)
        visible = (k_col >= jnp.where(q_row < 64, 0, 32)) & (
            k_col < jnp.where(q_row < 64, sl0, sl1 + 32)
        )
        for h in range(HALF // HD):
            head = slice(h * HD, (h + 1) * HD)
            query = query_acc[:, head].astype(BF16)
            scores = nt_dot(query, kv[0:64, head]) * HD ** (-0.5)
            scores = jnp.where(visible, scores, -1e30)
            scores = jnp.exp(scores - jnp.max(scores, axis=-1, keepdims=True))
            weights = (scores / jnp.sum(scores, axis=-1, keepdims=True)).astype(BF16)
            context[:, head] = dot(weights, kv[64:128, head]).astype(BF16)

    def project(*ns):
        if 0 in ns:
            net.recv("oyf", wo.at[:, :, 1 - c, :, more])
        net.recv(f"ozf{ns[0]}", wo.at[pl.ds(0, len(ns)), :, 1 - c, :, less])
        ks = [(z + (0, 7, 1, 6, 2, 5, 3, 4)[n]) % NZ for n in ns]
        products = [nt_dot(context[...], wo[k].reshape(256, HALF)) for k in ks]
        for k, product in zip(ks, products):
            mine, theirs = product[:, 0:128], product[:, 128:256]
            head_send[k] = jnp.where(s == 1, mine, theirs).astype(BF16)
            after[k] = tokens_ref[:, columns(k, s)].astype(F32) + jnp.where(s == 1, theirs, mine)
        for k in ks:
            net.send(head_send.at[k], head_recv.at[k], partner, "head", "head")

    def send_memory():
        theirs = memory_hbm.at[:, :, :, pl.ds(col1, HALF)]
        net.send(theirs, mem.at[s], partner, "memory", "memory")
        load_up.start()
        load_down.start()

    next(qy)
    next(qz)
    next(oy)
    next(oz)
    norm()
    next(qz)
    next(qy)
    slots()
    next(oy)
    next(qz)
    next(oz)
    next(qy)
    next(qy)
    next(oy)
    next(oy)
    send_memory()
    next(qz)
    next(oz)
    next(qy)
    next(qy)
    next(qz)
    next(oy)
    next(oy)
    next(qy)
    next(oz)
    next(qz)
    keys_values()
    query_y()
    next(oy)
    query_z()
    next(oz)
    attention()
    project(0)
    project(1, 2)
    project(3, 4)
    project(5, 6)
    next(oz)
    project(7)
    net.recv("head", head_recv)
    for k in range(NZ):
        after[k] += head_recv[k].astype(F32)

    values = jnp.concatenate([after[k] for k in range(NZ)], axis=1)
    mean = jnp.mean(values, axis=-1, keepdims=True)
    center = values - mean
    square = jnp.sum(center * center, axis=-1, keepdims=True)
    diagonal = iota((TOK, TOK), 0) == iota((TOK, TOK), 1)
    to_row = lambda column: jnp.sum(jnp.where(diagonal, column, 0.0), axis=0, keepdims=True)
    to_column = lambda row: jnp.sum(jnp.where(diagonal, row, 0.0), axis=1, keepdims=True)
    stat_send[...] = jnp.where(iota((8, TOK), 0) == 0, to_row(mean), to_row(square))
    net.send(stat_send, stat_recv, partner, "stat", "stat")
    net.recv("stat", stat_recv)
    mean_other, square_other = to_column(stat_recv[0:1, :]), to_column(stat_recv[1:2, :])
    gain = jnp.concatenate([moe_gain_ref[:, columns(k, s)] for k in range(NZ)], axis=1)
    gap = mean - mean_other
    spread = (square + square_other + gap * gap * (HALF / 2)) * (1.0 / D)
    mean = (mean + mean_other) * 0.5
    moe_in = (
        (values - mean) * lax.rsqrt(spread + 1e-05) * gain
    ).astype(BF16)

    own_z = pl.ds(pl.multiple_of(z * BLOCK, 16), BLOCK)
    own_chip = pl.ds(pl.multiple_of(chip * BLOCK, 16), BLOCK)
    z_blocks = [pl.ds(pl.multiple_of((z + d) % NZ * BLOCK, 16), BLOCK) for d in Z_STEPS]
    p_blocks = [pl.ds(pl.multiple_of(there * BLOCK, 16), BLOCK) for there in p_chips]

    def span(chunk):
        return pl.ds(chunk[0], chunk[1])

    def slabs(chunk):
        return range(chunk[0], chunk[0] + chunk[1])

    def side_by_side(parts):
        return jnp.concatenate(list(parts), axis=1)

    def spread(into, chunk, wide):
        for n, k in enumerate(slabs(chunk)):
            into[k] = wide[:, n * 128 : (n + 1) * 128].astype(into.dtype)

    def send_z(ch, chunk, source, into, name):
        into[span(chunk), own_z] = source[span(chunk), own_z]
        for block, peer in zip(z_blocks, z_peers):
            net.send(source.at[span(chunk), block], into.at[span(chunk), own_z], peer, name, f"{name}{ch}")

    def start_z(ch):
        chunk = DISPATCH[ch]
        columns_of = slice(chunk[0] * 128, (chunk[0] + chunk[1]) * 128)
        spread(z_send, chunk, dot(table[...], moe_in[:, columns_of]))
        send_z(ch, chunk, z_send, z_recv, "z")

    def add_up(cc, chunk):
        joined = side_by_side(rows[cc, k, ss] for k in slabs(chunk) for ss in range(2))
        depth = slice(chunk[0] * 256, (chunk[0] + chunk[1]) * 256)
        for n in range(HALF // 256):
            tile = slice(n * 256, (n + 1) * 256)
            product = dot(joined, w_up[depth, tile])
            if chunk[0] == 0:
                acc[cc, :, tile] = product
            else:
                acc[cc, :, tile] += product

    def finish_up(cc):
        hidden[cc] = jnp.maximum(acc[cc], 0.0).astype(BF16)

    load_up.wait()
    load_router.wait()
    for ch in range(len(DISPATCH)):
        start_z(ch)

    logit_send[...] = jnp.zeros_like(logit_send)
    logit_send[:, 0:EXPERTS] = nt_dot(
        moe_in, jnp.concatenate([w_router_ref[:, columns(k, s)] for k in range(NZ)], axis=1)
    )
    net.send(logit_send, logit_recv, partner, "logit", "logit")

    def like_plane(chunk):
        return z_recv.at[pl.ds(0, 5), pl.ds(0, 3 * BLOCK * chunk[1])]

    def arrived(ch):
        chunk = DISPATCH[ch]
        net.recv(f"p{ch}", like_plane(chunk))
        mine = rows.at[c, span(chunk)]
        net.send(mine, mine, sibling, "f", f"f{ch}")
        add_up(c, chunk)

    def passed_on(ch):
        net.recv(f"f{ch}", rows.at[1 - c, span(DISPATCH[ch])])
        add_up(1 - c, DISPATCH[ch])

    last = len(DISPATCH) - 1
    for ch, chunk in enumerate(DISPATCH):
        net.recv(f"z{ch}", z_recv.at[span(chunk), pl.ds(0, 7 * BLOCK)])
        spread(p_send, chunk, dot(perm_ref[...], side_by_side(z_recv[k] for k in slabs(chunk))))
        rows[c, span(chunk), s, own_chip] = p_send[span(chunk), own_chip]
        for block, peer in zip(p_blocks, p_peers):
            there = rows.at[c, span(chunk), s, own_chip]
            net.send(p_send.at[span(chunk), block], there, peer, "p", f"p{ch}")
        if ch >= 2:
            arrived(ch - 2)
        if ch >= 3:
            passed_on(ch - 3)
    arrived(last - 1)
    passed_on(last - 2)
    passed_on(last - 1)
    arrived(last)
    finish_up(c)
    passed_on(last)
    finish_up(1 - c)

    load_down.wait()

    def down(cc, ch, into):
        for k in slabs(RETURN[ch]):
            product = dot(hidden[cc], w_down[:, k * 256 : (k + 1) * 256]).astype(BF16)
            into[k, 0] = product[:, 0:128]
            into[k, 1] = product[:, 128:256]

    def give_part(ch):
        where = span(RETURN[ch])
        down(1 - c, ch, part_send)
        net.send(part_send.at[where], part_recv.at[where], sibling, "part", f"part{ch}")

    def start_back(ch):
        where = span(RETURN[ch])
        net.recv(f"part{ch}", part_recv.at[where])
        rp_send[where] = (part_own[where].astype(F32) + part_recv[where].astype(F32)).astype(BF16)
        rp_recv[where, s, own_chip] = rp_send[where, s, own_chip]
        for to_s, block, peer in zip(p_sections, p_blocks, p_peers):
            there = rp_recv.at[where, s, own_chip]
            net.send(rp_send.at[where, to_s, block], there, peer, "rp", f"rp{ch}")

    def back_over_z(ch):
        chunk = RETURN[ch]
        net.recv(f"rp{ch}", like_plane(chunk))
        both = [dot(perm_ref[...], side_by_side(rp_recv[k, ss] for k in slabs(chunk))) for ss in range(2)]
        spread(rz_send, chunk, both[0] + both[1])
        send_z(ch, chunk, rz_send, rz_recv, "rz")

    give_part(0)
    down(c, 0, part_own)
    for ch in range(len(RETURN)):
        if ch + 1 < len(RETURN):
            give_part(ch + 1)
        start_back(ch)
        if ch >= 3:
            back_over_z(ch - 3)
        if ch + 1 < len(RETURN):
            down(c, ch + 1, part_own)
    for ch in range(len(RETURN) - 3, len(RETURN)):
        back_over_z(ch)

    net.recv("logit", logit_recv)
    logits = (logit_send[...] + logit_recv[...])[:, 0:EXPERTS]
    picked0 = jnp.sum(jnp.where(pick0, logits, 0.0), axis=1, keepdims=True)
    picked1 = jnp.sum(jnp.where(pick1, logits, 0.0), axis=1, keepdims=True)
    gate0, gate1 = jax.nn.sigmoid(picked0 - picked1), jax.nn.sigmoid(picked1 - picked0)
    places = iota((TOK, SLOTS), 1).astype(F32)
    gates = jnp.where(places == from0, gate0, 0.0) + jnp.where(places == from1, gate1, 0.0)
    gates_high = gates.astype(BF16)
    gates_low = (gates - gates_high.astype(F32)).astype(BF16)

    for ch, chunk in enumerate(RETURN):
        net.recv(f"rz{ch}", rz_recv.at[span(chunk), pl.ds(0, 7 * BLOCK)])
        returned = side_by_side(rz_recv[k] for k in slabs(chunk))
        moe_out = dot(gates_high, returned) + dot(gates_low, returned)
        spread(out_send, chunk, side_by_side(after[k] for k in slabs(chunk)) + moe_out)
        net.send(out_send.at[span(chunk)], out_recv.at[span(chunk)], partner, "out", "out")
        for k in slabs(chunk):
            out_ref[:, columns(k, s)] = out_send[k]
    net.recv("out", out_recv)
    for k in range(NZ):
        out_ref[:, columns(k, 1 - s)] = out_recv[k]
    like_planes = rows.at[:, pl.ds(0, 5), :, pl.ds(0, 6 * BLOCK)]
    for name, like in (
        ("memory", mem.at[0]),
        ("head", head_send),
        ("stat", stat_send),
        ("logit", logit_send),
        ("z", z_send.at[:, pl.ds(0, 7 * BLOCK)]),
        ("p", like_planes),
        ("f", rows.at[c]),
        ("part", part_send),
        ("rp", like_planes),
        ("rz", rz_send.at[:, pl.ds(0, 7 * BLOCK)]),
        ("out", out_send),
    ):
        net.sent(name, like)
    for name, buf, cols in (("qz", wq, left), ("oz", wo, less)):
        net.sent(name + "p", buf.at[0, pl.ds(0, 7), c, :, cols])
        net.sent(name, buf.at[pl.ds(0, 7), :, c, :, cols])
        net.sent(name + "f", buf.at[:, :, c, :, cols])
    for name, buf, cols in (("qy", wq, right), ("oy", wo, more)):
        net.sent(name + "z", buf.at[pl.ds(0, 7), 0, c, :, cols])
        net.sent(name, buf.at[:, pl.ds(0, 7), c, :, cols])
        net.sent(name + "f", buf.at[:, :, c, :, cols])
    assert len(net.going) <= SENDS and len(net.coming) <= RECVS, (len(net.going), len(net.coming))


def permutation_kv():
    perm_kv = np.zeros((TOK, TOK), np.float32)
    for kind in range(2):
        for caption in range(2):
            for p in range(32):
                row = kind * 64 + caption * 32 + p
                perm_kv[row, p // 16 * 64 + caption * 32 + p % 16 * 2 + kind] = 1
    return jnp.asarray(perm_kv, BF16)


def body(
    tokens,
    memory,
    target_len,
    source_len,
    attn_gain,
    w_query,
    w_out,
    moe_gain,
    w_router,
    expert_ids,
    w_up,
    w_down,
):
    perm_kv = permutation_kv()
    vmem = pl.BlockSpec(memory_space=pltpu.VMEM)
    smem = pl.BlockSpec(memory_space=pltpu.SMEM)
    hbm = pl.BlockSpec(memory_space=pl.ANY)
    buf = lambda *shape: pltpu.VMEM(shape, BF16)
    wide = lambda *shape: pltpu.VMEM(shape, F32)
    return pl.pallas_call(
        kernel,
        out_shape=jax.ShapeDtypeStruct((TOK, D), BF16),
        in_specs=[hbm, hbm, smem, smem, vmem, hbm, hbm, vmem, hbm, vmem, vmem, hbm, hbm],
        out_specs=vmem,
        scratch_shapes=[
            buf(TOK, D),
            buf(EXPERTS, D),
            buf(8, 8, 2, 16, HALF),
            buf(8, 8, 2, 16, HALF),
            buf(D, HALF),
            buf(HALF, D),
            buf(2, 2, 16, 2, HALF),
            buf(TOK, HALF),
            buf(TOK, D),
            wide(TOK, HALF),
            buf(TOK, HALF),
            buf(NZ, TOK, 128),
            buf(NZ, TOK, 128),
            wide(NZ, TOK, 128),
            wide(8, TOK),
            wide(8, TOK),
            wide(TOK, 128),
            wide(TOK, 128),
            buf(SLOTS, TOK),
            buf(SLOTS, SLOTS),
            buf(NZ, SLOTS, 128),
            buf(NZ, SLOTS, 128),
            buf(NZ, SLOTS, 128),
            buf(2, NZ, 2, SLOTS, 128),
            wide(2, SLOTS, HALF),
            buf(2, SLOTS, HALF),
            buf(NZ, 2, SLOTS, 128),
            buf(NZ, 2, SLOTS, 128),
            buf(NZ, 2, SLOTS, 128),
            buf(NZ, 2, SLOTS, 128),
            buf(NZ, 2, SLOTS, 128),
            buf(NZ, SLOTS, 128),
            buf(NZ, SLOTS, 128),
            buf(NZ, TOK, 128),
            buf(NZ, TOK, 128),
            pltpu.SemaphoreType.DMA((SENDS,)),
            pltpu.SemaphoreType.DMA((RECVS,)),
            pltpu.SemaphoreType.DMA((7,)),
        ],
        compiler_params=pltpu.CompilerParams(
            collective_id=0, has_side_effects=True, vmem_limit_bytes=60 << 20
        ),
        cost_estimate=pl.CostEstimate(
            flops=8_000_000_000, bytes_accessed=12_000_000, transcendentals=300_000
        ),
    )(
        tokens,
        memory,
        target_len,
        source_len,
        attn_gain.reshape(1, D),
        w_query,
        w_out.T,
        moe_gain.reshape(1, D),
        w_router.T,
        expert_ids.T,
        perm_kv,
        w_up.reshape(D, HALF),
        w_down.reshape(HALF, D),
    )


def solution(mesh):
    return jax.shard_map(
        body,
        mesh=mesh,
        in_specs=(
            P("expert", None),
            P("expert", "section", None, None),
            P("expert"),
            P("expert"),
            P(),
            P("expert", "section"),
            P("section", "expert"),
            P(),
            P(),
            P("expert", None),
            P("expert", None, "section"),
            P("expert", "section", None),
        ),
        out_specs=P("expert", None),
        check_vma=False,
    )
```

```python
import math

import jax
import jax.numpy as jnp
import numpy as np
from jax import lax
from jax.experimental import pallas as pl
from jax.experimental.pallas import tpu as pltpu
from jax.sharding import PartitionSpec as P

MESH = pl.DeviceIdType.MESH
F32 = jnp.float32
BF16 = jnp.bfloat16

HD = 128
D = 2048
HALF = 1024
TOK = 128
CAP = 6
EXPERTS = 64
SLOTS = EXPERTS * CAP
BLOCK = 8 * CAP
NZ, NY, NX = 8, 4, 2
O_LEFT = 512
SENDS, RECVS = 23, 91
Z_STEPS = (4, 3, 5, 2, 6, 1, 7)
DISPATCH = ((0, 1), (1, 1), (2, 1), (3, 1), (4, 1), (5, 1), (6, 1), (7, 1))
RETURN = ((0, 1), (1, 1), (2, 1), (3, 1), (4, 1), (5, 1), (6, 1), (7, 1))
PLANE = ((2, 1), (1, 1), (3, 1), (2, 0), (0, 1), (1, 0), (3, 0))


def coords():
    s = lax.axis_index("section")
    e = lax.axis_index("expert")
    return s, e // 16, (e // 4) % 4, (e // 2) % 2, e % 2


def device(s, z, y, x, c):
    return (s, ((z * NY + y) * NX + x) * 2 + c)


class Net:
    def __init__(self, send_sem, recv_sem):
        self.send_sem, self.recv_sem = send_sem, recv_sem
        self.going, self.coming = {}, {}

    def send(self, src, dst, target, out, into):
        for groups, name in ((self.going, out), (self.coming, into)):
            groups.setdefault(name, [len(groups), 0])
            groups[name][1] += math.prod(src.shape)
        pltpu.make_async_remote_copy(
            src_ref=src,
            dst_ref=dst,
            send_sem=self.send_sem.at[self.going[out][0]],
            recv_sem=self.recv_sem.at[self.coming[into][0]],
            device_id=target,
            device_id_type=MESH,
        ).start()

    def recv(self, name, like):
        k, size = self.coming[name]
        assert size == math.prod(like.shape), name
        pltpu.make_async_copy(like, like, self.recv_sem.at[k]).wait()

    def sent(self, name, like):
        k, size = self.going[name]
        assert size == math.prod(like.shape), name
        pltpu.make_async_copy(like, like, self.send_sem.at[k]).wait()


def gather_z_last(net, buf, cols, name, groups):
    s, z, y, x, c = coords()
    view = lambda *idx: buf.at[(*idx, slice(None), cols)]
    sibling = device(s, z, y, x, 1 - c)
    up, down = device(s, (z + 1) % NZ, y, x, c), device(s, (z + 7) % NZ, y, x, c)

    def forward(n, k):
        block = view(k % NZ, slice(None), c)
        net.send(block, block, sibling, name + "f", name + "f" + groups[n])

    mine = view(z, y * 2 + x, c)
    for dy, dx in PLANE:
        net.send(mine, mine, device(s, z, (y + dy) % NY, (x + dx) % NX, c), name + "p", name + "p")
    yield
    net.recv(name + "p", view(z, pl.ds(0, 7), c))
    slab = view(z, slice(None), c)
    net.send(slab, slab, up, name, name + "u0")
    net.send(slab, slab, down, name, name + "d0")
    forward(0, z)
    for step in range(1, 4):
        yield
        for way, to, k, half in (("u", up, z + 8 - step, 0), ("d", down, z + step, 4)):
            block = view(k % NZ, slice(None), c)
            net.recv(f"{name}{way}{step - 1}", block)
            part = block if step < 3 else view(k % NZ, pl.ds(half, 4), c)
            net.send(part, part, to, name, f"{name}{way}{step}")
            forward(2 * step - (way == "u"), k)
    yield
    net.recv(name + "u3", view(0, pl.ds(0, 4), c))
    net.recv(name + "d3", view(0, pl.ds(0, 4), c))
    forward(7, z + 4)
    yield


def gather_y_last(net, buf, cols, name):
    s, z, y, x, c = coords()
    view = lambda *idx: buf.at[(*idx, slice(None), cols)]
    sibling = device(s, z, y, x, 1 - c)
    up, down = device(s, z, (y + 1) % NY, x, c), device(s, z, (y + 3) % NY, x, c)
    line = lambda dy, xx, zs=slice(None): view(zs, (y + dy) % NY * 2 + xx, c)

    def forward(dy, xx):
        net.send(line(dy, xx), line(dy, xx), sibling, name + "f", name + "f")

    def first(xx, which):
        for to in (up, down):
            net.send(line(0, xx), line(0, xx), to, name, name + which)
        forward(0, xx)

    def second(xx, which):
        net.recv(name + which, view(slice(None), pl.ds(0, 2), c))
        below, above = line(3, xx, pl.ds(0, 4)), line(1, xx, pl.ds(4, 4))
        net.send(below, below, up, name, name + which + "h")
        net.send(above, above, down, name, name + which + "h")
        forward(3, xx)
        forward(1, xx)

    def last(xx, which):
        net.recv(name + which + "h", view(slice(None), 0, c))
        forward(2, xx)

    mine = view(z, y * 2 + x, c)
    for d in Z_STEPS:
        net.send(mine, mine, device(s, (z + d) % NZ, y, x, c), name + "z", name + "z")
    yield
    net.recv(name + "z", view(pl.ds(0, 7), 0, c))
    first(x, "a")
    net.send(line(0, x), line(0, x), device(s, z, y, 1 - x, c), name, name + "x")
    yield
    second(x, "a")
    yield
    net.recv(name + "x", view(slice(None), 0, c))
    first(1 - x, "b")
    yield
    second(1 - x, "b")
    yield
    last(x, "a")
    yield
    last(1 - x, "b")
    yield


def iota(shape, dim):
    return lax.broadcasted_iota(jnp.int32, shape, dim)


def nt_dot(a, b):
    return lax.dot_general(a, b, (((1,), (1,)), ((), ())), preferred_element_type=F32)


def dot(a, b):
    return jnp.dot(a, b, preferred_element_type=F32)


def kernel(
    tokens_hbm,
    memory_hbm,
    target_len_ref,
    source_len_ref,
    attn_gain_ref,
    w_query_hbm,
    w_out_hbm,
    moe_gain_ref,
    w_router_hbm,
    ids_t_ref,
    perm_kv_ref,
    w_up_hbm,
    w_down_hbm,
    out_ref,
    tokens_ref,
    w_router_ref,
    wq,
    wo,
    w_up,
    w_down,
    mem,
    kv,
    normed,
    query_acc,
    context,
    head_send,
    head_recv,
    after,
    stat_send,
    stat_recv,
    logit_send,
    logit_recv,
    table,
    perm_ref,
    z_send,
    z_recv,
    p_send,
    rows,
    acc,
    hidden,
    part_send,
    part_recv,
    part_own,
    rp_send,
    rp_recv,
    rz_send,
    rz_recv,
    out_send,
    out_recv,
    send_sem,
    recv_sem,
    load_sem,
):
    s, z, y, x, c = coords()
    chip = y * 2 + x
    sibling, partner = device(s, z, y, x, 1 - c), device(1 - s, z, y, x, c)
    z_peers = [device(s, (z + d) % NZ, y, x, c) for d in Z_STEPS]
    p_peers, p_chips, p_sections = [], [], []
    for ds in (1, 0):
        for dy, dx in ((0, 0), *PLANE):
            if ds or dy or dx:
                to_s, to_y, to_x = (s + ds) % 2, (y + dy) % NY, (x + dx) % NX
                p_peers.append(device(to_s, z, to_y, to_x, c))
                p_chips.append(to_y * 2 + to_x)
                p_sections.append(to_s)

    col0 = pl.multiple_of(s * HALF, HALF)
    col1 = pl.multiple_of((1 - s) * HALF, HALF)
    load_up = pltpu.make_async_copy(w_up_hbm, w_up, load_sem.at[0])
    load_down = pltpu.make_async_copy(w_down_hbm, w_down, load_sem.at[1])
    load_mem = pltpu.make_async_copy(
        memory_hbm.at[:, :, :, pl.ds(col0, HALF)], mem.at[s], load_sem.at[2]
    )
    load_tokens = pltpu.make_async_copy(tokens_hbm, tokens_ref, load_sem.at[3])
    load_router = pltpu.make_async_copy(w_router_hbm, w_router_ref, load_sem.at[4])
    load_wq = pltpu.make_async_copy(w_query_hbm, wq.at[z, chip, c], load_sem.at[5])
    load_wo = pltpu.make_async_copy(w_out_hbm, wo.at[z, chip, c], load_sem.at[6])


    def columns(k, ss):
        return pl.ds(pl.multiple_of(k * 256 + ss * 128, 128), 128)

    barrier = pltpu.get_barrier_semaphore()
    peers = [sibling, *z_peers, *p_peers]
    for peer in peers:
        pl.semaphore_signal(barrier, inc=1, device_id=peer, device_id_type=MESH)
    for load in (load_wq, load_wo, load_tokens, load_mem, load_router):
        load.start()
    load_wq.wait()
    load_wo.wait()
    pl.semaphore_wait(barrier, len(peers))

    net = Net(send_sem, recv_sem)
    left, right = pl.ds(0, HALF // 2), pl.ds(HALF // 2, HALF // 2)
    less, more = pl.ds(0, O_LEFT), pl.ds(O_LEFT, HALF - O_LEFT)
    qz = gather_z_last(net, wq, left, "qz", [""] * NZ)
    qy = gather_y_last(net, wq, right, "qy")
    oz = gather_z_last(net, wo, less, "oz", ["0", "1", "1", "3", "3", "5", "5", "7"])
    oy = gather_y_last(net, wo, more, "oy")

    def norm():
        load_tokens.wait()
        values = tokens_ref[...].astype(F32)
        center = values - jnp.mean(values, axis=-1, keepdims=True)
        spread = jnp.mean(center * center, axis=-1, keepdims=True)
        normed[...] = (center * lax.rsqrt(spread + 1e-05) * attn_gain_ref[...]).astype(BF16)

    from0 = from1 = pick0 = pick1 = None

    def slots():
        nonlocal from0, from1, pick0, pick1
        tl0, tl1 = target_len_ref[0], target_len_ref[1]
        t = iota((1, TOK), 1)
        live = t < jnp.where(t < 64, tl0, tl1 + 64)
        i0, i1 = ids_t_ref[0:1, :], ids_t_ref[1:2, :]
        experts = iota((EXPERTS, TOK), 0)
        hit0, hit1 = (experts == i0) & live, (experts == i1) & live
        earlier = (iota((TOK, TOK), 0) < iota((TOK, TOK), 1)).astype(F32).astype(BF16)
        before = dot((hit0.astype(F32) + hit1.astype(F32)).astype(BF16), earlier)
        slot0 = jnp.sum(jnp.where(hit0, before, 0.0), axis=0, keepdims=True)
        slot1 = jnp.sum(jnp.where(hit1, before, 0.0), axis=0, keepdims=True)
        to0 = jnp.where(live, i0.astype(F32) * CAP + slot0, -1.0)
        to1 = jnp.where(live, i1.astype(F32) * CAP + slot1, -1.0)
        places = iota((SLOTS, TOK), 0).astype(F32)
        table[...] = ((places == to0) | (places == to1)).astype(F32).astype(BF16)

        t = iota((TOK, 1), 0)
        live = t < jnp.where(t < 64, tl0, tl1 + 64)
        eye = (iota((TOK, TOK), 0) == iota((TOK, TOK), 1)).astype(F32).astype(BF16)
        ids_col = nt_dot(eye, ids_t_ref[...].astype(F32).astype(BF16))
        i0, i1 = ids_col[:, 0:1], ids_col[:, 1:2]
        experts = iota((TOK, EXPERTS), 1).astype(F32)
        pick0, pick1 = experts == i0, experts == i1
        hit0, hit1 = pick0 & live, pick1 & live
        earlier = (iota((TOK, TOK), 1) < iota((TOK, TOK), 0)).astype(F32).astype(BF16)
        before = dot(earlier, (hit0.astype(F32) + hit1.astype(F32)).astype(BF16))
        slot0 = jnp.sum(jnp.where(hit0, before, 0.0), axis=1, keepdims=True)
        slot1 = jnp.sum(jnp.where(hit1, before, 0.0), axis=1, keepdims=True)
        from0 = jnp.where(live, i0 * CAP + slot0, -1.0)
        from1 = jnp.where(live, i1 * CAP + slot1, -1.0)

        i, j = iota((SLOTS, SLOTS), 0).astype(F32), iota((SLOTS, SLOTS), 1).astype(F32)
        block = jnp.floor((i + 0.5) * (1 / BLOCK))
        inner = i - block * BLOCK
        group = jnp.floor((inner + 0.5) * (1 / CAP))
        other = group * BLOCK + block * CAP + (inner - group * CAP)
        perm_ref[...] = (j == other).astype(F32).astype(BF16)

    def keys_values():
        load_mem.wait()
        net.recv("memory", mem.at[0])
        kv[...] = dot(perm_kv_ref[...], mem[...].reshape(TOK, HALF)).astype(BF16)

    def add_query(side):
        query_acc[:, side] = dot(normed[...], wq[:, :, :, :, side].reshape(D, HALF // 2))

    def query_z():
        net.recv("qzf", wq.at[:, :, 1 - c, :, left])
        add_query(slice(0, HALF // 2))

    def query_y():
        net.recv("qyf", wq.at[:, :, 1 - c, :, right])
        add_query(slice(HALF // 2, HALF))

    def attention():
        sl0, sl1 = source_len_ref[0], source_len_ref[1]
        q_row, k_col = iota((TOK, 64), 0), iota((TOK, 64), 1)
        visible = (k_col >= jnp.where(q_row < 64, 0, 32)) & (
            k_col < jnp.where(q_row < 64, sl0, sl1 + 32)
        )
        for h in range(HALF // HD):
            head = slice(h * HD, (h + 1) * HD)
            query = query_acc[:, head].astype(BF16)
            scores = nt_dot(query, kv[0:64, head]) * HD ** (-0.5)
            scores = jnp.where(visible, scores, -1e30)
            scores = jnp.exp(scores - jnp.max(scores, axis=-1, keepdims=True))
            weights = (scores / jnp.sum(scores, axis=-1, keepdims=True)).astype(BF16)
            context[:, head] = dot(weights, kv[64:128, head]).astype(BF16)

    def project(*ns):
        if 0 in ns:
            net.recv("oyf", wo.at[:, :, 1 - c, :, more])
        net.recv(f"ozf{ns[0]}", wo.at[pl.ds(0, len(ns)), :, 1 - c, :, less])
        ks = [(z + (0, 7, 1, 6, 2, 5, 3, 4)[n]) % NZ for n in ns]
        products = [nt_dot(context[...], wo[k].reshape(256, HALF)) for k in ks]
        for k, product in zip(ks, products):
            mine, theirs = product[:, 0:128], product[:, 128:256]
            head_send[k] = jnp.where(s == 1, mine, theirs).astype(BF16)
            after[k] = tokens_ref[:, columns(k, s)].astype(F32) + jnp.where(s == 1, theirs, mine)
        for k in ks:
            net.send(head_send.at[k], head_recv.at[k], partner, "head", "head")

    def send_memory():
        theirs = memory_hbm.at[:, :, :, pl.ds(col1, HALF)]
        net.send(theirs, mem.at[s], partner, "memory", "memory")
        load_up.start()
        load_down.start()

    next(qy)
    next(qz)
    next(oy)
    next(oz)
    norm()
    next(qz)
    next(qy)
    slots()
    next(oy)
    next(qz)
    next(oz)
    next(qy)
    next(qy)
    next(oy)
    next(oy)
    send_memory()
    next(qz)
    next(oz)
    next(qy)
    next(qy)
    next(qz)
    next(oy)
    next(oy)
    next(qy)
    keys_values()
    next(oz)
    query_y()
    next(qz)
    next(oy)
    query_z()
    next(oz)
    attention()
    project(0)
    project(1, 2)
    project(3, 4)
    project(5, 6)
    next(oz)
    project(7)
    net.recv("head", head_recv)
    for k in range(NZ):
        after[k] += head_recv[k].astype(F32)

    values = jnp.concatenate([after[k] for k in range(NZ)], axis=1)
    mean = jnp.mean(values, axis=-1, keepdims=True)
    center = values - mean
    square = jnp.sum(center * center, axis=-1, keepdims=True)
    diagonal = iota((TOK, TOK), 0) == iota((TOK, TOK), 1)
    to_row = lambda column: jnp.sum(jnp.where(diagonal, column, 0.0), axis=0, keepdims=True)
    to_column = lambda row: jnp.sum(jnp.where(diagonal, row, 0.0), axis=1, keepdims=True)
    stat_send[...] = jnp.where(iota((8, TOK), 0) == 0, to_row(mean), to_row(square))
    net.send(stat_send, stat_recv, partner, "stat", "stat")
    net.recv("stat", stat_recv)
    mean_other, square_other = to_column(stat_recv[0:1, :]), to_column(stat_recv[1:2, :])
    gain = jnp.concatenate([moe_gain_ref[:, columns(k, s)] for k in range(NZ)], axis=1)
    gap = mean - mean_other
    spread = (square + square_other + gap * gap * (HALF / 2)) * (1.0 / D)
    mean = (mean + mean_other) * 0.5
    moe_in = (
        (values - mean) * lax.rsqrt(spread + 1e-05) * gain
    ).astype(BF16)

    own_z = pl.ds(pl.multiple_of(z * BLOCK, 16), BLOCK)
    own_chip = pl.ds(pl.multiple_of(chip * BLOCK, 16), BLOCK)
    z_blocks = [pl.ds(pl.multiple_of((z + d) % NZ * BLOCK, 16), BLOCK) for d in Z_STEPS]
    p_blocks = [pl.ds(pl.multiple_of(there * BLOCK, 16), BLOCK) for there in p_chips]

    def span(chunk):
        return pl.ds(chunk[0], chunk[1])

    def slabs(chunk):
        return range(chunk[0], chunk[0] + chunk[1])

    def side_by_side(parts):
        return jnp.concatenate(list(parts), axis=1)

    def spread(into, chunk, wide):
        for n, k in enumerate(slabs(chunk)):
            into[k] = wide[:, n * 128 : (n + 1) * 128].astype(into.dtype)

    def send_z(ch, chunk, source, into, name):
        into[span(chunk), own_z] = source[span(chunk), own_z]
        for block, peer in zip(z_blocks, z_peers):
            net.send(source.at[span(chunk), block], into.at[span(chunk), own_z], peer, name, f"{name}{ch}")

    def start_z(ch):
        chunk = DISPATCH[ch]
        columns_of = slice(chunk[0] * 128, (chunk[0] + chunk[1]) * 128)
        spread(z_send, chunk, dot(table[...], moe_in[:, columns_of]))
        send_z(ch, chunk, z_send, z_recv, "z")

    def add_up(cc, chunk):
        joined = side_by_side(rows[cc, k, ss] for k in slabs(chunk) for ss in range(2))
        depth = slice(chunk[0] * 256, (chunk[0] + chunk[1]) * 256)
        for n in range(HALF // 256):
            tile = slice(n * 256, (n + 1) * 256)
            product = dot(joined, w_up[depth, tile])
            if chunk[0] == 0:
                acc[cc, :, tile] = product
            else:
                acc[cc, :, tile] += product

    def finish_up(cc):
        hidden[cc] = jnp.maximum(acc[cc], 0.0).astype(BF16)

    load_up.wait()
    load_router.wait()
    for ch in range(len(DISPATCH)):
        start_z(ch)

    logit_send[...] = jnp.zeros_like(logit_send)
    logit_send[:, 0:EXPERTS] = nt_dot(
        moe_in, jnp.concatenate([w_router_ref[:, columns(k, s)] for k in range(NZ)], axis=1)
    )
    net.send(logit_send, logit_recv, partner, "logit", "logit")

    def like_plane(chunk):
        return z_recv.at[pl.ds(0, 5), pl.ds(0, 3 * BLOCK * chunk[1])]

    def arrived(ch):
        chunk = DISPATCH[ch]
        net.recv(f"p{ch}", like_plane(chunk))
        mine = rows.at[c, span(chunk)]
        net.send(mine, mine, sibling, "f", f"f{ch}")
        add_up(c, chunk)

    def passed_on(ch):
        net.recv(f"f{ch}", rows.at[1 - c, span(DISPATCH[ch])])
        add_up(1 - c, DISPATCH[ch])

    last = len(DISPATCH) - 1
    for ch, chunk in enumerate(DISPATCH):
        net.recv(f"z{ch}", z_recv.at[span(chunk), pl.ds(0, 7 * BLOCK)])
        spread(p_send, chunk, dot(perm_ref[...], side_by_side(z_recv[k] for k in slabs(chunk))))
        rows[c, span(chunk), s, own_chip] = p_send[span(chunk), own_chip]
        for block, peer in zip(p_blocks, p_peers):
            there = rows.at[c, span(chunk), s, own_chip]
            net.send(p_send.at[span(chunk), block], there, peer, "p", f"p{ch}")
        if ch >= 2:
            arrived(ch - 2)
        if ch >= 3:
            passed_on(ch - 3)
    arrived(last - 1)
    passed_on(last - 2)
    passed_on(last - 1)
    arrived(last)
    finish_up(c)
    passed_on(last)
    finish_up(1 - c)

    load_down.wait()

    def down(cc, ch, into):
        for k in slabs(RETURN[ch]):
            product = dot(hidden[cc], w_down[:, k * 256 : (k + 1) * 256]).astype(BF16)
            into[k, 0] = product[:, 0:128]
            into[k, 1] = product[:, 128:256]

    def give_part(ch):
        where = span(RETURN[ch])
        down(1 - c, ch, part_send)
        net.send(part_send.at[where], part_recv.at[where], sibling, "part", f"part{ch}")

    def start_back(ch):
        where = span(RETURN[ch])
        net.recv(f"part{ch}", part_recv.at[where])
        rp_send[where] = (part_own[where].astype(F32) + part_recv[where].astype(F32)).astype(BF16)
        rp_recv[where, s, own_chip] = rp_send[where, s, own_chip]
        for to_s, block, peer in zip(p_sections, p_blocks, p_peers):
            there = rp_recv.at[where, s, own_chip]
            net.send(rp_send.at[where, to_s, block], there, peer, "rp", f"rp{ch}")

    def back_over_z(ch):
        chunk = RETURN[ch]
        net.recv(f"rp{ch}", like_plane(chunk))
        both = [dot(perm_ref[...], side_by_side(rp_recv[k, ss] for k in slabs(chunk))) for ss in range(2)]
        spread(rz_send, chunk, both[0] + both[1])
        send_z(ch, chunk, rz_send, rz_recv, "rz")

    give_part(0)
    down(c, 0, part_own)
    for ch in range(len(RETURN)):
        if ch + 1 < len(RETURN):
            give_part(ch + 1)
        start_back(ch)
        if ch >= 3:
            back_over_z(ch - 3)
        if ch + 1 < len(RETURN):
            down(c, ch + 1, part_own)
    for ch in range(len(RETURN) - 3, len(RETURN)):
        back_over_z(ch)

    net.recv("logit", logit_recv)
    logits = (logit_send[...] + logit_recv[...])[:, 0:EXPERTS]
    picked0 = jnp.sum(jnp.where(pick0, logits, 0.0), axis=1, keepdims=True)
    picked1 = jnp.sum(jnp.where(pick1, logits, 0.0), axis=1, keepdims=True)
    gate0, gate1 = jax.nn.sigmoid(picked0 - picked1), jax.nn.sigmoid(picked1 - picked0)
    places = iota((TOK, SLOTS), 1).astype(F32)
    gates = jnp.where(places == from0, gate0, 0.0) + jnp.where(places == from1, gate1, 0.0)
    gates_high = gates.astype(BF16)
    gates_low = (gates - gates_high.astype(F32)).astype(BF16)

    for ch, chunk in enumerate(RETURN):
        net.recv(f"rz{ch}", rz_recv.at[span(chunk), pl.ds(0, 7 * BLOCK)])
        returned = side_by_side(rz_recv[k] for k in slabs(chunk))
        moe_out = dot(gates_high, returned) + dot(gates_low, returned)
        spread(out_send, chunk, side_by_side(after[k] for k in slabs(chunk)) + moe_out)
        net.send(out_send.at[span(chunk)], out_recv.at[span(chunk)], partner, "out", "out")
        for k in slabs(chunk):
            out_ref[:, columns(k, s)] = out_send[k]
    net.recv("out", out_recv)
    for k in range(NZ):
        out_ref[:, columns(k, 1 - s)] = out_recv[k]
    like_planes = rows.at[:, pl.ds(0, 5), :, pl.ds(0, 6 * BLOCK)]
    for name, like in (
        ("memory", mem.at[0]),
        ("head", head_send),
        ("stat", stat_send),
        ("logit", logit_send),
        ("z", z_send.at[:, pl.ds(0, 7 * BLOCK)]),
        ("p", like_planes),
        ("f", rows.at[c]),
        ("part", part_send),
        ("rp", like_planes),
        ("rz", rz_send.at[:, pl.ds(0, 7 * BLOCK)]),
        ("out", out_send),
    ):
        net.sent(name, like)
    for name, buf, cols in (("qz", wq, left), ("oz", wo, less)):
        net.sent(name + "p", buf.at[0, pl.ds(0, 7), c, :, cols])
        net.sent(name, buf.at[pl.ds(0, 7), :, c, :, cols])
        net.sent(name + "f", buf.at[:, :, c, :, cols])
    for name, buf, cols in (("qy", wq, right), ("oy", wo, more)):
        net.sent(name + "z", buf.at[pl.ds(0, 7), 0, c, :, cols])
        net.sent(name, buf.at[:, pl.ds(0, 7), c, :, cols])
        net.sent(name + "f", buf.at[:, :, c, :, cols])
    assert len(net.going) <= SENDS and len(net.coming) <= RECVS, (len(net.going), len(net.coming))


def permutation_kv():
    perm_kv = np.zeros((TOK, TOK), np.float32)
    for kind in range(2):
        for caption in range(2):
            for p in range(32):
                row = kind * 64 + caption * 32 + p
                perm_kv[row, p // 16 * 64 + caption * 32 + p % 16 * 2 + kind] = 1
    return jnp.asarray(perm_kv, BF16)


def body(
    tokens,
    memory,
    target_len,
    source_len,
    attn_gain,
    w_query,
    w_out,
    moe_gain,
    w_router,
    expert_ids,
    w_up,
    w_down,
):
    perm_kv = permutation_kv()
    vmem = pl.BlockSpec(memory_space=pltpu.VMEM)
    smem = pl.BlockSpec(memory_space=pltpu.SMEM)
    hbm = pl.BlockSpec(memory_space=pl.ANY)
    buf = lambda *shape: pltpu.VMEM(shape, BF16)
    wide = lambda *shape: pltpu.VMEM(shape, F32)
    return pl.pallas_call(
        kernel,
        out_shape=jax.ShapeDtypeStruct((TOK, D), BF16),
        in_specs=[hbm, hbm, smem, smem, vmem, hbm, hbm, vmem, hbm, vmem, vmem, hbm, hbm],
        out_specs=vmem,
        scratch_shapes=[
            buf(TOK, D),
            buf(EXPERTS, D),
            buf(8, 8, 2, 16, HALF),
            buf(8, 8, 2, 16, HALF),
            buf(D, HALF),
            buf(HALF, D),
            buf(2, 2, 16, 2, HALF),
            buf(TOK, HALF),
            buf(TOK, D),
            wide(TOK, HALF),
            buf(TOK, HALF),
            buf(NZ, TOK, 128),
            buf(NZ, TOK, 128),
            wide(NZ, TOK, 128),
            wide(8, TOK),
            wide(8, TOK),
            wide(TOK, 128),
            wide(TOK, 128),
            buf(SLOTS, TOK),
            buf(SLOTS, SLOTS),
            buf(NZ, SLOTS, 128),
            buf(NZ, SLOTS, 128),
            buf(NZ, SLOTS, 128),
            buf(2, NZ, 2, SLOTS, 128),
            wide(2, SLOTS, HALF),
            buf(2, SLOTS, HALF),
            buf(NZ, 2, SLOTS, 128),
            buf(NZ, 2, SLOTS, 128),
            buf(NZ, 2, SLOTS, 128),
            buf(NZ, 2, SLOTS, 128),
            buf(NZ, 2, SLOTS, 128),
            buf(NZ, SLOTS, 128),
            buf(NZ, SLOTS, 128),
            buf(NZ, TOK, 128),
            buf(NZ, TOK, 128),
            pltpu.SemaphoreType.DMA((SENDS,)),
            pltpu.SemaphoreType.DMA((RECVS,)),
            pltpu.SemaphoreType.DMA((7,)),
        ],
        compiler_params=pltpu.CompilerParams(
            collective_id=0, has_side_effects=True, vmem_limit_bytes=60 << 20
        ),
        cost_estimate=pl.CostEstimate(
            flops=8_000_000_000, bytes_accessed=12_000_000, transcendentals=300_000
        ),
    )(
        tokens,
        memory,
        target_len,
        source_len,
        attn_gain.reshape(1, D),
        w_query,
        w_out.T,
        moe_gain.reshape(1, D),
        w_router.T,
        expert_ids.T,
        perm_kv,
        w_up.reshape(D, HALF),
        w_down.reshape(HALF, D),
    )


def solution(mesh):
    return jax.shard_map(
        body,
        mesh=mesh,
        in_specs=(
            P("expert", None),
            P("expert", "section", None, None),
            P("expert"),
            P("expert"),
            P(),
            P("expert", "section"),
            P("section", "expert"),
            P(),
            P(),
            P("expert", None),
            P("expert", None, "section"),
            P("expert", "section", None),
        ),
        out_specs=P("expert", None),
        check_vma=False,
    )
```
